256 devices in a mesh: row: 8 (over y, z_lo), col: 32 (over z_hi, x, core).
Axes of the slice: x: 4, y: 4, z: 8 (z_hi: 4, z_lo: 2; z = z_hi * 2 + z_lo), core: 2. Of those that a mesh axis runs over, the one named last changes fastest.
Arguments:
- positions: float32 [3, 524288], P(None, ('row', 'col')), may hold values from 0 to 173
- type_ids: int32 [524288], P(('row', 'col')), may hold values from 0 to 15
- type_params: float32 [2, 16], replicated, may hold values from 0.5 to 2
- pair_tiles: int32 [8, 32, 384, 2], P('row', 'col'), may hold values from 0 to 511, as said below
- pair_counts: int32 [8, 32], P('row', 'col'), may hold values from 48 to 384, as said below
Outputs:
- forces: float32 [3, 524288], P(None, ('row', 'col'))
The draws below stay inside these ranges and needn't reach their ends.
Inputs may be any that keep to these rules, and one draw needn't show every extreme that they name: `pair_tiles`: column 0 is a tile of the device's row block (below 512), column 1 a tile of its column set (below 128); slots at or after the device's count hold indices to be ignored. `pair_counts`: some device has all 384 slots live.
All inputs are finite; a program needn't handle non-finite values.
Results may differ from the reference program's by a relative error of at most 0.0003.
Values sent between devices are 32-bit elements; how exact they have to be, the bound alone decides.
A program may use at most 128 MiB of HBM per device.

```python
import math
import jax
import jax.numpy as jnp
from jax import lax

TILE = 128
NTYPES = 16
AT_DEV = 2048
MAXP = 384
ATOMS = 524288
N_ROW = 8
N_COL = 32


CELL_SIDE = 5.4


def cell_tables(key):
    cell_count = ATOMS // TILE
    tile_cell = jax.random.permutation(key, cell_count).astype(jnp.int32)
    cell_tile = jnp.zeros((cell_count,), jnp.int32).at[tile_cell].set(jnp.arange(cell_count, dtype=jnp.int32))
    return (tile_cell, cell_tile)


def cell_coords(cell_index):
    depth_cells = AT_DEV // TILE
    cell_x = cell_index % N_ROW
    cell_y = cell_index // N_ROW % N_COL
    cell_z = cell_index // (N_ROW * N_COL) % depth_cells
    return (cell_x, cell_y, cell_z)


def draw_positions(key, part):
    tile_cell, cell_tile = cell_tables(key)
    key = jax.random.fold_in(key, 13)
    tile_index = jnp.arange(ATOMS, dtype=jnp.int32) // TILE
    cell_index = tile_cell[tile_index]
    cell_x, cell_y, cell_z = cell_coords(cell_index)
    corner = jnp.stack([cell_x, cell_y, cell_z], axis=0).astype(jnp.float32)
    inside = jax.random.uniform(key, (3, ATOMS), jnp.float32)
    return ((corner + inside) * CELL_SIDE).astype(jnp.float32)


def draw_pair_tiles(key, part):
    tile_cell, cell_tile = cell_tables(key)
    key = jax.random.fold_in(key, 11)
    depth_cells = AT_DEV // TILE
    row_tiles = AT_DEV * N_COL // TILE
    row_pos = jnp.arange(N_ROW, dtype=jnp.int32)[:, None, None, None]
    col_pos = jnp.arange(N_COL, dtype=jnp.int32)[None, :, None, None]
    tile_pos = jnp.arange(row_tiles, dtype=jnp.int32)[None, None, :, None]
    steps_all = jnp.arange(27, dtype=jnp.int32)
    step_x = (steps_all % 3 - 1)[None, None, None, :]
    step_y = (steps_all // 3 % 3 - 1)[None, None, None, :]
    step_z = (steps_all // 9 - 1)[None, None, None, :]
    global_tile = row_pos * row_tiles + tile_pos
    cell_x, cell_y, cell_z = cell_coords(tile_cell[global_tile])
    near_x = cell_x + step_x
    near_y = cell_y + step_y
    near_z = cell_z + step_z
    inside = (near_x >= 0) & (near_x < N_ROW) & (near_y >= 0) & (near_y < N_COL) & (near_z >= 0) & (near_z < depth_cells)
    near_x = jnp.clip(near_x, 0, N_ROW - 1)
    near_y = jnp.clip(near_y, 0, N_COL - 1)
    near_z = jnp.clip(near_z, 0, depth_cells - 1)
    near_cell = near_x + N_ROW * (near_y + N_COL * near_z)
    near_tile = cell_tile[near_cell]
    near_row = near_tile // (N_COL * depth_cells)
    near_col = near_tile // depth_cells % N_COL
    near_depth = near_tile % depth_cells
    valid = inside & (near_col == col_pos)
    column_tile = near_row * depth_cells + near_depth
    total = row_tiles * 27
    valid = valid.reshape(N_ROW, N_COL, total)
    column_tile = jnp.broadcast_to(column_tile, (N_ROW, N_COL, row_tiles, 27)).reshape(N_ROW, N_COL, total)
    device_keys = jax.random.split(key, N_ROW * N_COL)
    ranks = jax.vmap(lambda one_key: jax.random.permutation(one_key, total))(device_keys).reshape(N_ROW, N_COL, total).astype(jnp.int32)
    scores = jnp.where(valid, ranks, ranks + total)
    order = jnp.argsort(scores, axis=-1, stable=True).astype(jnp.int32)
    live_total = jnp.maximum(jnp.sum(valid.astype(jnp.int32), axis=-1), 1)
    slot_pick = jnp.arange(MAXP, dtype=jnp.int32)[None, None, :] % live_total[:, :, None]
    chosen = jnp.take_along_axis(order, slot_pick, axis=-1)
    first_tile = chosen // 27
    second_tile = jnp.take_along_axis(column_tile, chosen, axis=-1)
    return jnp.stack([first_tile, second_tile], axis=3).astype(jnp.int32)


def draw_pair_counts(key, part):
    key = jax.random.fold_in(key, 12)
    shift_key, busy_key = jax.random.split(key)
    shifts = jax.random.randint(shift_key, (N_ROW * N_COL,), 0, 4)
    busiest = jax.random.randint(busy_key, (), 0, N_ROW * N_COL)
    shifts = jnp.where(jnp.arange(N_ROW * N_COL) == busiest, 0, shifts)
    counts = jnp.right_shift(jnp.full((N_ROW * N_COL,), MAXP, jnp.int32), shifts.astype(jnp.int32))
    return counts.reshape(N_ROW, N_COL).astype(jnp.int32)


def touch_ends(array, key, least, largest):
    extent = array.shape
    index_at = [jax.random.randint(jax.random.fold_in(key, axis), (), 0, extent[axis]) for axis in range(len(extent))]
    array = array.at[tuple(index_at)].set(least)
    longest = extent.index(max(extent))
    index_at[longest] = (index_at[longest] + 1) % extent[longest]
    return array.at[tuple(index_at)].set(largest)


def setup_inputs(seed: int = 0) -> dict:
    streams_of = jax.random.split(jax.random.key(seed), 6)
    positions = draw_positions(jax.random.fold_in(streams_of[5], 71), 0)
    type_ids = touch_ends(jax.random.randint(streams_of[1], (ATOMS,), 0, NTYPES), jax.random.fold_in(streams_of[1], 1), 0, NTYPES - 1).astype(jnp.int32)
    type_params = jnp.clip(jnp.exp(jax.random.uniform(streams_of[2], (2, NTYPES), jnp.float32, math.log(0.5), math.log(2.0))), 0.5, 2.0)
    pair_tiles = draw_pair_tiles(jax.random.fold_in(streams_of[5], 71), 0)
    pair_counts = draw_pair_counts(jax.random.fold_in(streams_of[5], 71), 0)
    return dict(positions=positions, type_ids=type_ids, type_params=type_params, pair_tiles=pair_tiles, pair_counts=pair_counts)


STRENGTH = 1.0
CUTOFF_SQ = 6.25
pair_batch = 32

def atom_table(positions, type_ids, type_params):
    onehot = (type_ids[None, :] == jnp.arange(NTYPES, dtype=jnp.int32)[:, None]).astype(jnp.float32)
    per_atom = jnp.dot(type_params, onehot, precision=lax.Precision.HIGHEST)
    return jnp.concatenate([positions, jnp.sqrt(per_atom[0:1]), per_atom[1:2]], axis=0)

def tile_split(atom_data):
    return atom_data.reshape(atom_data.shape[0], atom_data.shape[1] // TILE, TILE).transpose(1, 0, 2)

def tile_join(tiled):
    return tiled.transpose(1, 0, 2).reshape(tiled.shape[1], tiled.shape[0] * tiled.shape[2])

def pair_block(row_tiles, col_tiles, pair_list, live_slot):
    left_tile = row_tiles[pair_list[:, 0]]
    right_tile = col_tiles[pair_list[:, 1]]
    offset_vec = left_tile[:, :3, :, None] - right_tile[:, :3, None, :]
    dist_sq = lax.optimization_barrier(jnp.sum(offset_vec * offset_vec, axis=1))
    well_depth = left_tile[:, 3, :, None] * right_tile[:, 3, None, :]
    well_width = 0.5 * (left_tile[:, 4, :, None] + right_tile[:, 4, None, :])
    inverse_sq = 1.0 / (well_width * well_width)
    falloff = jnp.exp(-dist_sq * inverse_sq)
    cutoff_term = jnp.maximum(1.0 - dist_sq / CUTOFF_SQ, 0.0)
    radial_slope = STRENGTH * well_depth * falloff * (-cutoff_term * cutoff_term * inverse_sq - 2.0 * cutoff_term / CUTOFF_SQ)
    radial_slope = jnp.where(live_slot[:, None, None], radial_slope, 0.0)
    pair_force = 2.0 * radial_slope[:, None] * offset_vec
    return (-lax.optimization_barrier(jnp.sum(pair_force, axis=3)), lax.optimization_barrier(jnp.sum(pair_force, axis=2)))

def evaluate(row_tiles, col_tiles, pair_tiles, slot_count, blocks):
    row_zero = jnp.zeros((row_tiles.shape[0], 3, TILE), jnp.float32)
    col_zero = jnp.zeros((col_tiles.shape[0], 3, TILE), jnp.float32)

    def block_step(block_id, totals):
        first_slot = jnp.asarray(block_id, jnp.int32) * pair_batch
        pair_list = lax.dynamic_slice_in_dim(pair_tiles, first_slot, pair_batch, 0)
        live_slot = first_slot + jnp.arange(pair_batch, dtype=jnp.int32) < slot_count
        on_rows, on_cols = pair_block(row_tiles, col_tiles, pair_list, live_slot)
        return (totals[0].at[pair_list[:, 0]].add(on_rows), totals[1].at[pair_list[:, 1]].add(on_cols))
    return lax.fori_loop(0, blocks, block_step, (row_zero, col_zero))

def reference(positions, type_ids, type_params, pair_tiles, pair_counts):
    atom_grid = atom_table(positions, type_ids, type_params).reshape(5, N_ROW, N_COL, AT_DEV)

    def device_step(totals, flat_index):
        row_index = (flat_index // N_COL).astype(jnp.int32)
        col_index = (flat_index % N_COL).astype(jnp.int32)
        row_data = lax.dynamic_index_in_dim(atom_grid, row_index, 1, keepdims=False).reshape(5, N_COL * AT_DEV)
        col_data = lax.dynamic_index_in_dim(atom_grid, col_index, 2, keepdims=False).reshape(5, N_ROW * AT_DEV)
        row_force, col_force = evaluate(tile_split(row_data), tile_split(col_data), pair_tiles[row_index, col_index], pair_counts[row_index, col_index], MAXP // pair_batch)
        row_part = tile_join(row_force).reshape(3, 1, N_COL, AT_DEV)
        col_part = tile_join(col_force).reshape(3, N_ROW, 1, AT_DEV)
        zero = jnp.int32(0)
        old_rows = lax.dynamic_slice(totals, (zero, row_index, zero, zero), (3, 1, N_COL, AT_DEV))
        totals = lax.dynamic_update_slice(totals, old_rows + row_part, (zero, row_index, zero, zero))
        old_cols = lax.dynamic_slice(totals, (zero, zero, col_index, zero), (3, N_ROW, 1, AT_DEV))
        totals = lax.dynamic_update_slice(totals, old_cols + col_part, (zero, zero, col_index, zero))
        return (totals, None)
    totals, _ = lax.scan(device_step, jnp.zeros((3, N_ROW, N_COL, AT_DEV), jnp.float32), jnp.arange(N_ROW * N_COL, dtype=jnp.int32))
    return totals.reshape(3, N_ROW * N_COL * AT_DEV)
```

```python
import functools
import math

import jax
import jax.numpy as jnp
from jax import lax
from jax.experimental import pallas as pl
from jax.experimental.pallas import tpu as pltpu
from jax.sharding import PartitionSpec as P

TILE = 128
NTYPES = 16
CUTOFF_SQ = 6.25
LOG2E = math.log2(math.e)
KAPPA = 2.0 / (CUTOFF_SQ * LOG2E)
UNROLL = 2
ROW_TILES = 512
COL_TILES = 128
F32 = jnp.float32
BF16 = jnp.bfloat16


def pieces(value):
    high = value.astype(BF16).astype(F32)
    rest = value - high
    middle = rest.astype(BF16).astype(F32)
    return high, middle, rest, rest - middle


def distance_stack(value, order):
    high, middle, _, low = pieces(value)
    part = {"h": high, "m": middle, "l": low}
    return [jnp.concatenate([part[order[k]], part[order[k + 1]]], axis=0).astype(BF16) for k in (0, 2, 4)]


def moment_stack(value, upper):
    high, _, rest, low = pieces(value)
    return jnp.concatenate([jnp.where(upper, high, rest), jnp.where(upper, low, 0.0)], axis=0).astype(BF16)


def force_kernel(count_ref, tiles_ref, params_ref, row_ref, col_ref, row_out, col_out, feat, mom, cen, vel, acc_row, acc_col):
    sub = lax.broadcasted_iota(jnp.int32, (8, TILE), 0)
    quad = sub & 3
    upper = sub < 4
    subf = sub.astype(F32)
    unit = jnp.where(sub == 4, 1.0, 0.0)

    eye = lax.broadcasted_iota(jnp.int32, (NTYPES, NTYPES), 0) == lax.broadcasted_iota(jnp.int32, (NTYPES, NTYPES), 1)
    width = params_ref[1:2, :]
    width_sub = jnp.sum(jnp.where(eye, width, 0.0), axis=1, keepdims=True)
    total = 0.5 * (width_sub + width)
    table = (CUTOFF_SQ * LOG2E) / (total * total)
    t_high, t_mid, _, t_low = pieces(table)
    table48 = jnp.concatenate([t_high, t_mid, t_low], axis=0).astype(BF16)
    root = jnp.sqrt(params_ref[0:1, :])
    root_sub = jnp.sum(jnp.where(eye, root, 0.0), axis=1, keepdims=True)
    root_a = jnp.broadcast_to(root_sub[0:8], (8, TILE))
    root_b = jnp.broadcast_to(root_sub[8:16], (8, TILE))

    def typed(kind):
        hit_a = subf == kind
        hit_b = subf + 8.0 == kind
        onehot = jnp.concatenate([jnp.where(hit_a, 1.0, 0.0), jnp.where(hit_b, 1.0, 0.0)], axis=0).astype(BF16)
        depth = jnp.sum(jnp.where(hit_a, root_a, 0.0) + jnp.where(hit_b, root_b, 0.0), axis=0, keepdims=True)
        return onehot, jnp.broadcast_to(depth, (8, TILE))

    def spread(x, y, z, last):
        return jnp.where(quad == 0, x, jnp.where(quad == 1, y, jnp.where(quad == 2, z, last)))

    def wide(ref, dev, comp, lane):
        return jnp.broadcast_to(ref[dev, comp : comp + 1, pl.ds(lane, TILE)], (8, TILE))

    zero_pack = jnp.zeros((16, TILE), BF16)

    def prepare(b):
        dev = b // 16
        lane = pl.multiple_of((b % 16) * TILE, TILE)
        x, y, z, kind = (wide(col_ref, dev, k, lane) for k in range(4))
        here = spread(x, y, z, 0.0)
        centre = jnp.sum(here, axis=1, keepdims=True) * (1.0 / TILE)
        cen[b] = jnp.broadcast_to(centre, (8, TILE))
        v = here - centre
        square = jnp.where(sub < 3, v * v, 0.0)
        norm = jnp.sum(square, axis=0, keepdims=True)
        onehot, depth = typed(kind)
        z8 = jnp.where(sub < 3, v * (2.0 / CUTOFF_SQ), jnp.where(sub == 3, 1.0, jnp.where(sub == 4, norm * (-1.0 / CUTOFF_SQ), 0.0)))
        first = distance_stack(z8, "hmlhmh")
        second = jnp.dot(table48, onehot, preferred_element_type=F32).astype(BF16)
        stack = jnp.concatenate(first + [second, zero_pack, zero_pack], axis=0)
        feat[b] = stack.T
        xz = jnp.where(quad == 3, 1.0, v)
        mom[b] = moment_stack(xz * depth, upper)
        vel[b] = jnp.where(sub == 3, depth * KAPPA, v)

    @pl.loop(0, COL_TILES, step=4)
    def _(b0):
        for k in range(4):
            prepare(b0 + k)

    acc_row[...] = jnp.zeros_like(acc_row)
    acc_col[...] = jnp.zeros_like(acc_col)

    count = count_ref[0, 0]

    def fold(out):
        first = out[0:8]
        return first + pltpu.roll(first, 4, 0) + out[8:16]

    def pair(slot):
        live = slot < count
        a = jnp.where(live, tiles_ref[0, slot], 0)
        b = jnp.where(live, tiles_ref[1, slot], 0)
        a_to = pl.multiple_of(jnp.where(live, a, ROW_TILES) * 8, 8)
        b_to = pl.multiple_of(jnp.where(live, b, COL_TILES) * 8, 8)
        owner = a // 16
        dev = (owner & 1) * 16 + ((owner >> 1) & 3) * 4 + (owner >> 3)
        lane = pl.multiple_of((a & 15) * TILE, TILE)
        x, y, z = (wide(row_ref, dev, k, lane) - jnp.broadcast_to(cen[b, k : k + 1, :], (8, TILE)) for k in range(3))
        kind = wide(row_ref, dev, 3, lane)
        onehot, depth = typed(kind)
        q = 1.0 - (x * x + y * y + z * z) * (1.0 / CUTOFF_SQ)
        xz = spread(x, y, z, 1.0)
        z8 = jnp.where(sub < 3, xz, jnp.where(sub == 3, q, unit))
        blocks = distance_stack(z8, "hhhmml")
        zeros3 = [zero_pack] * 3
        near = jnp.concatenate(blocks + zeros3 + [zero_pack] * 2, axis=0)
        kinds = jnp.concatenate(zeros3 + [onehot] * 3 + [zero_pack] * 2, axis=0)
        both = jnp.dot(feat[b], jnp.concatenate([near, kinds], axis=1), preferred_element_type=F32)
        c = jnp.maximum(both[:, :TILE], 0.0)
        k = both[:, TILE:]
        u = c * k
        g = (c * (u + 2.0 * LOG2E)) * jnp.exp2(u - k)
        g_high = g.astype(BF16)
        g_low = (g - g_high.astype(F32)).astype(BF16)
        xj = mom[b]
        xi = moment_stack(xz * depth, upper)
        to_i = fold(jnp.dot(xj, g_high, preferred_element_type=F32) + jnp.dot(xj, g_low, preferred_element_type=F32))
        across = (((1,), (1,)), ((), ()))
        to_j = fold(
            lax.dot_general(xi, g_high, across, preferred_element_type=F32)
            + lax.dot_general(xi, g_low, across, preferred_element_type=F32)
        )
        weight = jnp.broadcast_to(to_i[3:4], (8, TILE))
        on_i = (xz * weight - to_i) * (depth * KAPPA)
        return a_to, b_to, on_i, to_j

    @pl.loop(0, pl.cdiv(count, UNROLL))
    def _(step):
        done = [pair(step * UNROLL + k) for k in range(UNROLL)]
        for a_to, b_to, on_i, to_j in done:
            acc_row[pl.ds(a_to, 8), :] += on_i
            acc_col[pl.ds(b_to, 8), :] += to_j

    @pl.loop(0, COL_TILES, step=4)
    def _(b0):
        for k in range(4):
            b = b0 + k
            at = pl.multiple_of(b * 8, 8)
            got = acc_col[pl.ds(at, 8), :]
            v = vel[b]
            weight = jnp.broadcast_to(got[3:4], (8, TILE))
            depth = jnp.broadcast_to(v[3:4], (8, TILE))
            acc_col[pl.ds(at, 8), :] = (v * weight - got) * depth

    for q in range(32):
        slot = (q & 1) * 16 + ((q >> 1) & 3) * 4 + (q >> 3)
        for c in range(3):
            row_out[slot, c * 16 : c * 16 + 16, :] = acc_row[pl.ds(q * 128 + c, 16, stride=8), :]
    for p in range(8):
        for c in range(3):
            col_out[p, c * 16 : c * 16 + 16, :] = acc_col[pl.ds(p * 128 + c, 16, stride=8), :]


def forces_of(count, tiles, params, row_data, col_data):
    smem = pl.BlockSpec(memory_space=pltpu.SMEM)
    vmem = pl.BlockSpec(memory_space=pltpu.VMEM)
    return pl.pallas_call(
        force_kernel,
        out_shape=(jax.ShapeDtypeStruct((32, 48, TILE), F32), jax.ShapeDtypeStruct((8, 48, TILE), F32)),
        in_specs=[smem, smem, vmem, vmem, vmem],
        out_specs=(vmem, vmem),
        scratch_shapes=[
            pltpu.VMEM((COL_TILES, TILE, TILE), BF16),
            pltpu.VMEM((COL_TILES, 16, TILE), BF16),
            pltpu.VMEM((COL_TILES, 8, TILE), F32),
            pltpu.VMEM((COL_TILES, 8, TILE), F32),
            pltpu.VMEM(((ROW_TILES + 1) * 8, TILE), F32),
            pltpu.VMEM(((COL_TILES + 1) * 8, TILE), F32),
        ],
        compiler_params=pltpu.CompilerParams(vmem_limit_bytes=40 * 1024 * 1024),
        name="pair_forces",
    )(count, tiles, params, row_data, col_data)


MESH = pl.DeviceIdType.MESH
HALF = 1024


def place():
    p, q = lax.axis_index("row"), lax.axis_index("col")
    return p // 2, p % 2, q // 8, (q // 2) % 4, q % 2


def device(y, zl, zh, x, core):
    return (y * 2 + zl, zh * 8 + x * 2 + core)


def neighbours(y, zl, zh, x, core):
    ring = lambda v, d: (v + d + 4) % 4
    return dict(
        z_up=device(y, zl, ring(zh, 1), x, core),
        z_down=device(y, zl, ring(zh, -1), x, core),
        x_up=device(y, zl, zh, ring(x, 1), core),
        x_down=device(y, zl, zh, ring(x, -1), core),
        y_up=device(ring(y, 1), zl, zh, x, core),
        y_down=device(ring(y, -1), zl, zh, x, core),
        twin=device(y, zl, zh, x, 1 - core),
        pal=device(y, 1 - zl, zh, x, core),
    )


def greet(near):
    barrier = pltpu.get_barrier_semaphore()
    for target in near.values():
        pl.semaphore_signal(barrier, inc=1, device_id=target, device_id_type=MESH)
    pl.semaphore_wait(barrier, len(near))


class Copies:
    def __init__(self, near, send_sem, recv_sem):
        self.near, self.send_sem, self.recv_sem = near, send_sem, recv_sem
        self.number = 0
        self.started = []

    def start(self, source, target, to):
        k = self.number
        self.number += 1
        copy = pltpu.make_async_remote_copy(
            src_ref=source,
            dst_ref=target,
            send_sem=self.send_sem.at[k],
            recv_sem=self.recv_sem.at[k],
            device_id=self.near[to],
            device_id_type=MESH,
        )
        copy.start()
        self.started.append(copy)
        return copy

    def finish(self):
        for copy in self.started:
            copy.wait_send()


GATHER_COPIES = 48
SCATTER_COPIES = 32


def gather_kernel(pos_ref, type_ref, row_ref, col_ref, send_sem, recv_sem):
    y, zl, zh, x, core = place()
    near = neighbours(y, zl, zh, x, core)
    ring = lambda v, d: (v + d + 4) % 4
    at = lambda xx, zz: core * 16 + xx * 4 + zz
    mine = at(x, zh)
    col_at = lambda yy, ll: yy * 2 + ll
    col_mine = col_at(y, zl)
    for ref, slot in ((row_ref, mine), (col_ref, col_mine)):
        ref[slot, 0:3, :] = pos_ref[...]
        for k in range(16):
            ref[slot, 3:4, k * TILE : (k + 1) * TILE] = type_ref[k : k + 1, :].astype(F32)
    greet(near)
    net = Copies(near, send_sem, recv_sem)
    low, high = pl.ds(0, HALF), pl.ds(HALF, HALF)

    def whole(ref, slot, to):
        return net.start(ref.at[slot], ref.at[slot], to)

    def part(ref, slot, lanes, to):
        return net.start(ref.at[slot, :, lanes], ref.at[slot, :, lanes], to)

    z_from_down = whole(row_ref, mine, "z_up")
    z_from_up = whole(row_ref, mine, "z_down")
    pal_copy = whole(col_ref, col_mine, "pal")
    y_from_down = [whole(col_ref, col_mine, "y_up")]
    y_from_up = [whole(col_ref, col_mine, "y_down")]
    x_from_down, x_from_up = [], []

    def along_x(slot):
        x_from_down.append(whole(row_ref, slot, "x_up"))
        x_from_up.append(whole(row_ref, slot, "x_down"))

    along_x(mine)
    twins = [whole(row_ref, mine, "twin")]
    z_from_down.wait_recv()
    z_low = part(row_ref, at(x, ring(zh, -1)), low, "z_up")
    along_x(at(x, ring(zh, -1)))
    z_from_up.wait_recv()
    z_high = part(row_ref, at(x, ring(zh, 1)), high, "z_down")
    along_x(at(x, ring(zh, 1)))
    pal_copy.wait_recv()
    y_from_down.append(whole(col_ref, col_at(y, 1 - zl), "y_up"))
    y_from_up.append(whole(col_ref, col_at(y, 1 - zl), "y_down"))
    twins.append(whole(row_ref, at(x, ring(zh, -1)), "twin"))
    twins.append(whole(row_ref, at(x, ring(zh, 1)), "twin"))

    x_low, x_high = [], []

    def onward(k, zz):
        x_from_down[k].wait_recv()
        x_low.append(part(row_ref, at(ring(x, -1), zz), low, "x_up"))
        x_from_up[k].wait_recv()
        x_high.append(part(row_ref, at(ring(x, 1), zz), high, "x_down"))
        twins.append(whole(row_ref, at(ring(x, -1), zz), "twin"))
        twins.append(whole(row_ref, at(ring(x, 1), zz), "twin"))

    onward(0, zh)
    z_low.wait_recv()
    z_high.wait_recv()
    along_x(at(x, ring(zh, 2)))
    twins.append(whole(row_ref, at(x, ring(zh, 2)), "twin"))

    y_low, y_high = [], []
    for k, ll in ((0, zl), (1, 1 - zl)):
        y_from_down[k].wait_recv()
        y_low.append(part(col_ref, col_at(ring(y, -1), ll), low, "y_up"))
        y_from_up[k].wait_recv()
        y_high.append(part(col_ref, col_at(ring(y, 1), ll), high, "y_down"))

    onward(1, ring(zh, -1))
    onward(2, ring(zh, 1))
    onward(3, ring(zh, 2))
    for k, d in enumerate((0, -1, 1, 2)):
        x_low[k].wait_recv()
        x_high[k].wait_recv()
        twins.append(whole(row_ref, at(ring(x, 2), ring(zh, d)), "twin"))
    for copy in y_low + y_high + twins:
        copy.wait_recv()
    net.finish()


def gather(positions, kinds):
    vmem = pl.BlockSpec(memory_space=pltpu.VMEM)
    return pl.pallas_call(
        gather_kernel,
        out_shape=(jax.ShapeDtypeStruct((32, 4, 2048), F32), jax.ShapeDtypeStruct((8, 4, 2048), F32)),
        in_specs=[vmem, vmem],
        out_specs=(vmem, vmem),
        scratch_shapes=[pltpu.SemaphoreType.DMA((GATHER_COPIES,)), pltpu.SemaphoreType.DMA((GATHER_COPIES,))],
        compiler_params=pltpu.CompilerParams(
            collective_id=0, has_side_effects=True, vmem_limit_bytes=16 * 1024 * 1024
        ),
        name="gather_atoms",
    )(positions, kinds)


def scatter_kernel(row_ref, col_ref, out_ref, from_twin, row_sum, x_half, x_whole, z_half, z_whole, y_half, y_whole, pal_in, col_sum, send_sem, recv_sem):
    y, zl, zh, x, core = place()
    near = neighbours(y, zl, zh, x, core)
    ring = lambda v, d: (v + d + 4) % 4
    greet(near)
    net = Copies(near, send_sem, recv_sem)

    offsets = (2, 1, -1, 0)
    twins = {}
    for d in offsets:
        there = pl.ds((1 - core) * 16 + ring(x, d) * 4, 4)
        twins[d] = net.start(row_ref.at[there], from_twin.at[pl.ds(ring(x, d) * 4, 4)], "twin")

    far = ring(y, 2) * 2
    y_low = net.start(col_ref.at[pl.ds(far, 1)], y_half.at[pl.ds(0, 1)], "y_up")
    y_high = net.start(col_ref.at[pl.ds(far + 1, 1)], y_half.at[pl.ds(1, 1)], "y_down")

    def join(d):
        twins[d].wait_recv()
        rows = pl.ds(ring(x, d) * 4, 4)
        row_sum[rows] = row_ref[pl.ds(core * 16 + ring(x, d) * 4, 4)] + from_twin[rows]

    join(2)
    far_x = ring(x, 2) * 4
    x_low = net.start(row_sum.at[pl.ds(far_x, 2)], x_half.at[pl.ds(0, 2)], "x_up")
    x_high = net.start(row_sum.at[pl.ds(far_x + 2, 2)], x_half.at[pl.ds(2, 2)], "x_down")

    y_low.wait_recv()
    up = ring(y, 1) * 2
    col_sum[0] = col_ref[up] + y_half[0]
    y_up0 = net.start(col_sum.at[0], y_whole.at[0], "y_up")
    y_up1 = net.start(col_ref.at[up + 1], y_whole.at[1], "y_up")
    y_high.wait_recv()
    down = ring(y, -1) * 2
    col_sum[1] = col_ref[down + 1] + y_half[1]
    y_down0 = net.start(col_ref.at[down], y_whole.at[2], "y_down")
    y_down1 = net.start(col_sum.at[1], y_whole.at[3], "y_down")

    join(1)
    up_x = ring(x, 1) * 4
    x_up1 = net.start(row_sum.at[pl.ds(up_x + 2, 2)], x_whole.at[pl.ds(2, 2)], "x_up")
    join(-1)
    down_x = ring(x, -1) * 4
    x_down0 = net.start(row_sum.at[pl.ds(down_x, 2)], x_whole.at[pl.ds(4, 2)], "x_down")
    x_low.wait_recv()
    row_sum[pl.ds(up_x, 2)] += x_half[0:2]
    x_up0 = net.start(row_sum.at[pl.ds(up_x, 2)], x_whole.at[pl.ds(0, 2)], "x_up")
    x_high.wait_recv()
    row_sum[pl.ds(down_x + 2, 2)] += x_half[2:4]
    x_down1 = net.start(row_sum.at[pl.ds(down_x + 2, 2)], x_whole.at[pl.ds(6, 2)], "x_down")
    join(0)

    for copy in (y_up0, y_up1, y_down0, y_down1):
        copy.wait_recv()
    here = y * 2
    col_sum[2] = col_ref[here + 1 - zl] + y_whole[1 - zl] + y_whole[3 - zl]
    pal_copy = net.start(col_sum.at[2], pal_in, "pal")
    col_sum[3] = col_ref[here + zl] + y_whole[zl] + y_whole[2 + zl]

    for copy in (x_up1, x_down0, x_up0, x_down1):
        copy.wait_recv()
    base = x * 4
    row_sum[pl.ds(base, 4)] += x_whole[0:4] + x_whole[4:8]

    z_far = base + ring(zh, 2)
    z_low = net.start(row_sum.at[z_far, pl.ds(0, 24)], z_half.at[0], "z_up")
    z_high = net.start(row_sum.at[z_far, pl.ds(24, 24)], z_half.at[1], "z_down")
    z_up, z_down = base + ring(zh, 1), base + ring(zh, -1)
    z_up1 = net.start(row_sum.at[z_up, pl.ds(24, 24)], z_whole.at[0, pl.ds(24, 24)], "z_up")
    z_down0 = net.start(row_sum.at[z_down, pl.ds(0, 24)], z_whole.at[1, pl.ds(0, 24)], "z_down")
    z_low.wait_recv()
    row_sum[z_up, 0:24] += z_half[0]
    z_up0 = net.start(row_sum.at[z_up, pl.ds(0, 24)], z_whole.at[0, pl.ds(0, 24)], "z_up")
    z_high.wait_recv()
    row_sum[z_down, 24:48] += z_half[1]
    z_down1 = net.start(row_sum.at[z_down, pl.ds(24, 24)], z_whole.at[1, pl.ds(24, 24)], "z_down")
    pal_copy.wait_recv()
    for copy in (z_up1, z_down0, z_up0, z_down1):
        copy.wait_recv()
    col_sum[3] = col_sum[3] + pal_in[...] + row_sum[base + zh] + z_whole[0] + z_whole[1]
    for c in range(3):
        for k in range(16):
            out_ref[c : c + 1, k * TILE : (k + 1) * TILE] = col_sum[3, c * 16 + k : c * 16 + k + 1, :]
    net.finish()


def scatter(row_part, col_part):
    vmem = pl.BlockSpec(memory_space=pltpu.VMEM)
    block = lambda n: pltpu.VMEM((n, 48, TILE), F32)
    return pl.pallas_call(
        scatter_kernel,
        out_shape=jax.ShapeDtypeStruct((3, 2048), F32),
        in_specs=[vmem, vmem],
        out_specs=vmem,
        scratch_shapes=[
            block(16),
            block(16),
            block(4),
            block(8),
            pltpu.VMEM((2, 24, TILE), F32),
            block(2),
            block(2),
            block(4),
            pltpu.VMEM((48, TILE), F32),
            block(4),
            pltpu.SemaphoreType.DMA((SCATTER_COPIES,)),
            pltpu.SemaphoreType.DMA((SCATTER_COPIES,)),
        ],
        compiler_params=pltpu.CompilerParams(
            collective_id=1, has_side_effects=True, vmem_limit_bytes=16 * 1024 * 1024
        ),
        name="scatter_forces",
    )(row_part, col_part)


def shards(positions, type_ids, type_params, pair_tiles, pair_counts):
    row_data, col_data = gather(positions, type_ids.reshape(16, TILE))
    tiles = pair_tiles[0, 0].T
    row_part, col_part = forces_of(pair_counts, tiles, type_params, row_data, col_data)
    return scatter(row_part, col_part)


def solution(mesh):
    placed = (
        P(None, ("row", "col")),
        P(("row", "col")),
        P(),
        P("row", "col", None, None),
        P("row", "col"),
    )
    return jax.shard_map(
        shards, mesh=mesh, in_specs=placed, out_specs=P(None, ("row", "col")), check_vma=False
    )
```

```python
import functools
import math

import jax
import jax.numpy as jnp
from jax import lax
from jax.experimental import pallas as pl
from jax.experimental.pallas import tpu as pltpu
from jax.sharding import PartitionSpec as P

TILE = 128
NTYPES = 16
CUTOFF_SQ = 6.25
LOG2E = math.log2(math.e)
KAPPA = 2.0 / (CUTOFF_SQ * LOG2E)
UNROLL = 16
PREPARE = 16
ROW_TILES = 512
COL_TILES = 128
F32 = jnp.float32
BF16 = jnp.bfloat16


def pieces(value):
    high = value.astype(BF16).astype(F32)
    rest = value - high
    middle = rest.astype(BF16).astype(F32)
    return high, middle, rest, rest - middle


def distance_stack(value, order):
    high, middle, _, low = pieces(value)
    part = {"h": high, "m": middle, "l": low}
    return [jnp.concatenate([part[order[k]], part[order[k + 1]]], axis=0).astype(BF16) for k in (0, 2, 4)]


def moment_stack(value, upper):
    high, _, rest, low = pieces(value)
    return jnp.concatenate([jnp.where(upper, high, rest), jnp.where(upper, low, 0.0)], axis=0).astype(BF16)


def force_kernel(count_ref, tiles_ref, params_ref, row_ref, col_ref, row_out, col_out, feat, mom, cen, vel, acc_row, acc_col, slope, mine, offset, scale):
    sub = lax.broadcasted_iota(jnp.int32, (8, TILE), 0)
    quad = sub & 3
    upper = sub < 4
    subf = sub.astype(F32)
    unit = jnp.where(sub == 4, 1.0, 0.0)

    eye = lax.broadcasted_iota(jnp.int32, (NTYPES, NTYPES), 0) == lax.broadcasted_iota(jnp.int32, (NTYPES, NTYPES), 1)
    width = params_ref[1:2, :]
    width_sub = jnp.sum(jnp.where(eye, width, 0.0), axis=1, keepdims=True)
    total = 0.5 * (width_sub + width)
    table = (CUTOFF_SQ * LOG2E) / (total * total)
    t_high, t_mid, _, t_low = pieces(table)
    table48 = jnp.concatenate([t_high, t_mid, t_low], axis=0).astype(BF16)
    root = jnp.sqrt(params_ref[0:1, :])
    root_sub = jnp.sum(jnp.where(eye, root, 0.0), axis=1, keepdims=True)
    root_a = jnp.broadcast_to(root_sub[0:8], (8, TILE))
    root_b = jnp.broadcast_to(root_sub[8:16], (8, TILE))

    def typed(kind):
        hit_a = subf == kind
        hit_b = subf + 8.0 == kind
        onehot = jnp.concatenate([jnp.where(hit_a, 1.0, 0.0), jnp.where(hit_b, 1.0, 0.0)], axis=0).astype(BF16)
        depth = jnp.sum(jnp.where(hit_a, root_a, 0.0) + jnp.where(hit_b, root_b, 0.0), axis=0, keepdims=True)
        return onehot, jnp.broadcast_to(depth, (8, TILE))

    def spread(x, y, z, last):
        return jnp.where(quad == 0, x, jnp.where(quad == 1, y, jnp.where(quad == 2, z, last)))

    def wide(ref, dev, comp, lane):
        return jnp.broadcast_to(ref[dev, comp : comp + 1, pl.ds(lane, TILE)], (8, TILE))

    zero_pack = jnp.zeros((16, TILE), BF16)

    def prepare(b):
        dev = b // 16
        lane = pl.multiple_of((b % 16) * TILE, TILE)
        x, y, z, kind = (wide(col_ref, dev, k, lane) for k in range(4))
        here = spread(x, y, z, 0.0)
        centre = jnp.sum(here, axis=1, keepdims=True) * (1.0 / TILE)
        cen[b] = jnp.broadcast_to(centre, (8, TILE))
        v = here - centre
        square = jnp.where(sub < 3, v * v, 0.0)
        norm = jnp.sum(square, axis=0, keepdims=True)
        onehot, depth = typed(kind)
        z8 = jnp.where(sub < 3, v * (2.0 / CUTOFF_SQ), jnp.where(sub == 3, 1.0, jnp.where(sub == 4, norm * (-1.0 / CUTOFF_SQ), 0.0)))
        first = distance_stack(z8, "hmlhmh")
        second = jnp.dot(table48, onehot, preferred_element_type=F32).astype(BF16)
        stack = jnp.concatenate(first + [second, zero_pack, zero_pack], axis=0)
        feat[b] = stack.T
        xz = jnp.where(quad == 3, 1.0, v)
        mom[b] = moment_stack(xz * depth, upper)
        vel[b] = jnp.where(sub == 3, depth * KAPPA, v)
        acc_row[pl.ds(pl.multiple_of(b * 32, 32), 32), :] = jnp.zeros((32, TILE), F32)
        acc_col[pl.ds(pl.multiple_of(b * 8, 8), 8), :] = jnp.zeros((8, TILE), F32)

    @pl.loop(0, COL_TILES, step=PREPARE)
    def _(b0):
        for k in range(PREPARE):
            prepare(b0 + k)

    slope[...] = jnp.zeros_like(slope)
    mine[...] = jnp.zeros_like(mine)
    offset[...] = jnp.zeros_like(offset)
    scale[...] = jnp.zeros_like(scale)

    count = count_ref[0, 0]

    def fold(out):
        first = out[0:8]
        return first + pltpu.roll(first, 4, 0) + out[8:16]

    zeros3 = [zero_pack] * 3
    zeros2 = [zero_pack] * 2

    def names(slot):
        live = (slot >= 0) & (slot < count)
        at = jnp.clip(slot, 0, count - 1)
        return live, tiles_ref[0, at], tiles_ref[1, at]

    def spread_out(slot, k):
        _, a, b = names(slot)
        owner = a // 16
        dev = (owner & 1) * 16 + ((owner >> 1) & 3) * 4 + (owner >> 3)
        lane = pl.multiple_of((a & 15) * TILE, TILE)
        x, y, z = (wide(row_ref, dev, c, lane) - jnp.broadcast_to(cen[b, c : c + 1, :], (8, TILE)) for c in range(3))
        kind = wide(row_ref, dev, 3, lane)
        onehot, depth = typed(kind)
        q = 1.0 - (x * x + y * y + z * z) * (1.0 / CUTOFF_SQ)
        xz = spread(x, y, z, 1.0)
        z8 = jnp.where(sub < 3, xz, jnp.where(sub == 3, q, unit))
        near = jnp.concatenate(distance_stack(z8, "hhhmml") + zeros3 + zeros2, axis=0)
        kinds = jnp.concatenate(zeros3 + [onehot] * 3 + zeros2, axis=0)
        both = jnp.dot(feat[b], jnp.concatenate([near, kinds], axis=1), preferred_element_type=F32)
        c = jnp.maximum(both[:, :TILE], 0.0)
        decay = both[:, TILE:]
        u = c * decay
        g = (c * (u + 2.0 * LOG2E)) * jnp.exp2(u - decay)
        g_high = g.astype(BF16)
        g_low = (g - g_high.astype(F32)).astype(BF16)
        slope[k, 0:TILE, :] = g_high
        slope[k, TILE : 2 * TILE, :] = g_low
        mine[k] = moment_stack(xz * depth, upper)
        offset[k] = xz
        scale[k] = depth * KAPPA

    def gather_in(slot, k):
        live, a, b = names(slot)
        a_to = pl.multiple_of(jnp.where(live, a, ROW_TILES) * 8, 8)
        b_to = pl.multiple_of(jnp.where(live, b, COL_TILES) * 8, 8)
        sides = jnp.concatenate([mom[b], mine[k]], axis=0)
        g = slope[k]
        across = jnp.concatenate([g[:TILE].T, g[TILE:].T], axis=0)
        out = jnp.dot(
            jnp.concatenate([sides, sides], axis=1),
            jnp.concatenate([g, across], axis=1),
            preferred_element_type=F32,
        )
        to_i = fold(out[0:16, :TILE])
        to_j = fold(out[16:32, TILE:])
        weight = jnp.broadcast_to(to_i[3:4], (8, TILE))
        on_i = (offset[k] * weight - to_i) * scale[k]
        return a_to, b_to, on_i, to_j

    @pl.loop(0, pl.cdiv(count, UNROLL) + 1)
    def _(step):
        done = [gather_in((step - 1) * UNROLL + k, k) for k in range(UNROLL)]
        for k in range(UNROLL):
            spread_out(step * UNROLL + k, k)
        for a_to, b_to, on_i, to_j in done:
            acc_row[pl.ds(a_to, 8), :] += on_i
            acc_col[pl.ds(b_to, 8), :] += to_j

    @pl.loop(0, COL_TILES, step=4)
    def _(b0):
        for k in range(4):
            b = b0 + k
            at = pl.multiple_of(b * 8, 8)
            got = acc_col[pl.ds(at, 8), :]
            v = vel[b]
            weight = jnp.broadcast_to(got[3:4], (8, TILE))
            depth = jnp.broadcast_to(v[3:4], (8, TILE))
            acc_col[pl.ds(at, 8), :] = (v * weight - got) * depth

    for q in range(32):
        slot = (q & 1) * 16 + ((q >> 1) & 3) * 4 + (q >> 3)
        for c in range(3):
            row_out[slot, c * 16 : c * 16 + 16, :] = acc_row[pl.ds(q * 128 + c, 16, stride=8), :]
    for p in range(8):
        for c in range(3):
            col_out[p, c * 16 : c * 16 + 16, :] = acc_col[pl.ds(p * 128 + c, 16, stride=8), :]


def forces_of(count, tiles, params, row_data, col_data):
    smem = pl.BlockSpec(memory_space=pltpu.SMEM)
    vmem = pl.BlockSpec(memory_space=pltpu.VMEM)
    return pl.pallas_call(
        force_kernel,
        out_shape=(jax.ShapeDtypeStruct((32, 48, TILE), F32), jax.ShapeDtypeStruct((8, 48, TILE), F32)),
        in_specs=[smem, smem, vmem, vmem, vmem],
        out_specs=(vmem, vmem),
        scratch_shapes=[
            pltpu.VMEM((COL_TILES, TILE, TILE), BF16),
            pltpu.VMEM((COL_TILES, 16, TILE), BF16),
            pltpu.VMEM((COL_TILES, 8, TILE), F32),
            pltpu.VMEM((COL_TILES, 8, TILE), F32),
            pltpu.VMEM(((ROW_TILES + 1) * 8, TILE), F32),
            pltpu.VMEM(((COL_TILES + 1) * 8, TILE), F32),
            pltpu.VMEM((UNROLL, 2 * TILE, TILE), BF16),
            pltpu.VMEM((UNROLL, 16, TILE), BF16),
            pltpu.VMEM((UNROLL, 8, TILE), F32),
            pltpu.VMEM((UNROLL, 8, TILE), F32),
        ],
        compiler_params=pltpu.CompilerParams(vmem_limit_bytes=40 * 1024 * 1024),
        name="pair_forces",
    )(count, tiles, params, row_data, col_data)


MESH = pl.DeviceIdType.MESH
HALF = 1024


def place():
    p, q = lax.axis_index("row"), lax.axis_index("col")
    return p // 2, p % 2, q // 8, (q // 2) % 4, q % 2


def device(y, zl, zh, x, core):
    return (y * 2 + zl, zh * 8 + x * 2 + core)


def neighbours(y, zl, zh, x, core):
    ring = lambda v, d: (v + d + 4) % 4
    return dict(
        z_up=device(y, zl, ring(zh, 1), x, core),
        z_down=device(y, zl, ring(zh, -1), x, core),
        x_up=device(y, zl, zh, ring(x, 1), core),
        x_down=device(y, zl, zh, ring(x, -1), core),
        y_up=device(ring(y, 1), zl, zh, x, core),
        y_down=device(ring(y, -1), zl, zh, x, core),
        twin=device(y, zl, zh, x, 1 - core),
        pal=device(y, 1 - zl, zh, x, core),
    )


def greet(near):
    barrier = pltpu.get_barrier_semaphore()
    for target in near.values():
        pl.semaphore_signal(barrier, inc=1, device_id=target, device_id_type=MESH)
    pl.semaphore_wait(barrier, len(near))


class Copies:
    def __init__(self, near, send_sem, recv_sem):
        self.near, self.send_sem, self.recv_sem = near, send_sem, recv_sem
        self.number = 0
        self.started = []

    def start(self, source, target, to):
        k = self.number
        self.number += 1
        copy = pltpu.make_async_remote_copy(
            src_ref=source,
            dst_ref=target,
            send_sem=self.send_sem.at[k],
            recv_sem=self.recv_sem.at[k],
            device_id=self.near[to],
            device_id_type=MESH,
        )
        copy.start()
        self.started.append(copy)
        return copy

    def finish(self):
        for copy in self.started:
            copy.wait_send()


GATHER_COPIES = 48
SCATTER_COPIES = 32


def gather_kernel(pos_ref, type_ref, row_ref, col_ref, send_sem, recv_sem):
    y, zl, zh, x, core = place()
    near = neighbours(y, zl, zh, x, core)
    ring = lambda v, d: (v + d + 4) % 4
    at = lambda xx, zz: core * 16 + xx * 4 + zz
    mine = at(x, zh)
    col_at = lambda yy, ll: yy * 2 + ll
    col_mine = col_at(y, zl)
    for ref, slot in ((row_ref, mine), (col_ref, col_mine)):
        ref[slot, 0:3, :] = pos_ref[...]
        for k in range(16):
            ref[slot, 3:4, k * TILE : (k + 1) * TILE] = type_ref[k : k + 1, :].astype(F32)
    greet(near)
    net = Copies(near, send_sem, recv_sem)
    low, high = pl.ds(0, HALF), pl.ds(HALF, HALF)

    def whole(ref, slot, to):
        return net.start(ref.at[slot], ref.at[slot], to)

    def part(ref, slot, lanes, to):
        return net.start(ref.at[slot, :, lanes], ref.at[slot, :, lanes], to)

    z_from_down = whole(row_ref, mine, "z_up")
    z_from_up = whole(row_ref, mine, "z_down")
    pal_copy = whole(col_ref, col_mine, "pal")
    y_from_down = [whole(col_ref, col_mine, "y_up")]
    y_from_up = [whole(col_ref, col_mine, "y_down")]
    x_from_down, x_from_up = [], []

    def along_x(slot):
        x_from_down.append(whole(row_ref, slot, "x_up"))
        x_from_up.append(whole(row_ref, slot, "x_down"))

    along_x(mine)
    twins = [whole(row_ref, mine, "twin")]
    z_from_down.wait_recv()
    z_low = part(row_ref, at(x, ring(zh, -1)), low, "z_up")
    along_x(at(x, ring(zh, -1)))
    z_from_up.wait_recv()
    z_high = part(row_ref, at(x, ring(zh, 1)), high, "z_down")
    along_x(at(x, ring(zh, 1)))
    pal_copy.wait_recv()
    y_from_down.append(whole(col_ref, col_at(y, 1 - zl), "y_up"))
    y_from_up.append(whole(col_ref, col_at(y, 1 - zl), "y_down"))
    twins.append(whole(row_ref, at(x, ring(zh, -1)), "twin"))
    twins.append(whole(row_ref, at(x, ring(zh, 1)), "twin"))

    x_low, x_high = [], []

    def onward(k, zz):
        x_from_down[k].wait_recv()
        x_low.append(part(row_ref, at(ring(x, -1), zz), low, "x_up"))
        x_from_up[k].wait_recv()
        x_high.append(part(row_ref, at(ring(x, 1), zz), high, "x_down"))
        twins.append(whole(row_ref, at(ring(x, -1), zz), "twin"))
        twins.append(whole(row_ref, at(ring(x, 1), zz), "twin"))

    onward(0, zh)
    z_low.wait_recv()
    z_high.wait_recv()
    along_x(at(x, ring(zh, 2)))
    twins.append(whole(row_ref, at(x, ring(zh, 2)), "twin"))

    y_low, y_high = [], []
    for k, ll in ((0, zl), (1, 1 - zl)):
        y_from_down[k].wait_recv()
        y_low.append(part(col_ref, col_at(ring(y, -1), ll), low, "y_up"))
        y_from_up[k].wait_recv()
        y_high.append(part(col_ref, col_at(ring(y, 1), ll), high, "y_down"))

    onward(1, ring(zh, -1))
    onward(2, ring(zh, 1))
    onward(3, ring(zh, 2))
    for k, d in enumerate((0, -1, 1, 2)):
        x_low[k].wait_recv()
        x_high[k].wait_recv()
        twins.append(whole(row_ref, at(ring(x, 2), ring(zh, d)), "twin"))
    for copy in y_low + y_high + twins:
        copy.wait_recv()
    net.finish()


def gather(positions, kinds):
    vmem = pl.BlockSpec(memory_space=pltpu.VMEM)
    return pl.pallas_call(
        gather_kernel,
        out_shape=(jax.ShapeDtypeStruct((32, 4, 2048), F32), jax.ShapeDtypeStruct((8, 4, 2048), F32)),
        in_specs=[vmem, vmem],
        out_specs=(vmem, vmem),
        scratch_shapes=[pltpu.SemaphoreType.DMA((GATHER_COPIES,)), pltpu.SemaphoreType.DMA((GATHER_COPIES,))],
        compiler_params=pltpu.CompilerParams(
            collective_id=0, has_side_effects=True, vmem_limit_bytes=16 * 1024 * 1024
        ),
        name="gather_atoms",
    )(positions, kinds)


def scatter_kernel(row_ref, col_ref, out_ref, from_twin, row_sum, x_half, x_whole, z_half, z_whole, y_half, y_whole, pal_in, col_sum, send_sem, recv_sem):
    y, zl, zh, x, core = place()
    near = neighbours(y, zl, zh, x, core)
    ring = lambda v, d: (v + d + 4) % 4
    greet(near)
    net = Copies(near, send_sem, recv_sem)

    offsets = (2, 1, -1, 0)
    twins = {}
    for d in offsets:
        there = pl.ds((1 - core) * 16 + ring(x, d) * 4, 4)
        twins[d] = net.start(row_ref.at[there], from_twin.at[pl.ds(ring(x, d) * 4, 4)], "twin")

    far = ring(y, 2) * 2
    y_low = net.start(col_ref.at[pl.ds(far, 1)], y_half.at[pl.ds(0, 1)], "y_up")
    y_high = net.start(col_ref.at[pl.ds(far + 1, 1)], y_half.at[pl.ds(1, 1)], "y_down")

    def join(d):
        twins[d].wait_recv()
        rows = pl.ds(ring(x, d) * 4, 4)
        row_sum[rows] = row_ref[pl.ds(core * 16 + ring(x, d) * 4, 4)] + from_twin[rows]

    join(2)
    far_x = ring(x, 2) * 4
    x_low = net.start(row_sum.at[pl.ds(far_x, 2)], x_half.at[pl.ds(0, 2)], "x_up")
    x_high = net.start(row_sum.at[pl.ds(far_x + 2, 2)], x_half.at[pl.ds(2, 2)], "x_down")

    y_low.wait_recv()
    up = ring(y, 1) * 2
    col_sum[0] = col_ref[up] + y_half[0]
    y_up0 = net.start(col_sum.at[0], y_whole.at[0], "y_up")
    y_up1 = net.start(col_ref.at[up + 1], y_whole.at[1], "y_up")
    y_high.wait_recv()
    down = ring(y, -1) * 2
    col_sum[1] = col_ref[down + 1] + y_half[1]
    y_down0 = net.start(col_ref.at[down], y_whole.at[2], "y_down")
    y_down1 = net.start(col_sum.at[1], y_whole.at[3], "y_down")

    join(1)
    up_x = ring(x, 1) * 4
    x_up1 = net.start(row_sum.at[pl.ds(up_x + 2, 2)], x_whole.at[pl.ds(2, 2)], "x_up")
    join(-1)
    down_x = ring(x, -1) * 4
    x_down0 = net.start(row_sum.at[pl.ds(down_x, 2)], x_whole.at[pl.ds(4, 2)], "x_down")
    x_low.wait_recv()
    row_sum[pl.ds(up_x, 2)] += x_half[0:2]
    x_up0 = net.start(row_sum.at[pl.ds(up_x, 2)], x_whole.at[pl.ds(0, 2)], "x_up")
    x_high.wait_recv()
    row_sum[pl.ds(down_x + 2, 2)] += x_half[2:4]
    x_down1 = net.start(row_sum.at[pl.ds(down_x + 2, 2)], x_whole.at[pl.ds(6, 2)], "x_down")
    join(0)

    for copy in (y_up0, y_up1, y_down0, y_down1):
        copy.wait_recv()
    here = y * 2
    col_sum[2] = col_ref[here + 1 - zl] + y_whole[1 - zl] + y_whole[3 - zl]
    pal_copy = net.start(col_sum.at[2], pal_in, "pal")
    col_sum[3] = col_ref[here + zl] + y_whole[zl] + y_whole[2 + zl]

    for copy in (x_up1, x_down0, x_up0, x_down1):
        copy.wait_recv()
    base = x * 4
    row_sum[pl.ds(base, 4)] += x_whole[0:4] + x_whole[4:8]

    z_far = base + ring(zh, 2)
    z_low = net.start(row_sum.at[z_far, pl.ds(0, 24)], z_half.at[0], "z_up")
    z_high = net.start(row_sum.at[z_far, pl.ds(24, 24)], z_half.at[1], "z_down")
    z_up, z_down = base + ring(zh, 1), base + ring(zh, -1)
    z_up1 = net.start(row_sum.at[z_up, pl.ds(24, 24)], z_whole.at[0, pl.ds(24, 24)], "z_up")
    z_down0 = net.start(row_sum.at[z_down, pl.ds(0, 24)], z_whole.at[1, pl.ds(0, 24)], "z_down")
    z_low.wait_recv()
    row_sum[z_up, 0:24] += z_half[0]
    z_up0 = net.start(row_sum.at[z_up, pl.ds(0, 24)], z_whole.at[0, pl.ds(0, 24)], "z_up")
    z_high.wait_recv()
    row_sum[z_down, 24:48] += z_half[1]
    z_down1 = net.start(row_sum.at[z_down, pl.ds(24, 24)], z_whole.at[1, pl.ds(24, 24)], "z_down")
    pal_copy.wait_recv()
    for copy in (z_up1, z_down0, z_up0, z_down1):
        copy.wait_recv()
    col_sum[3] = col_sum[3] + pal_in[...] + row_sum[base + zh] + z_whole[0] + z_whole[1]
    for c in range(3):
        for k in range(16):
            out_ref[c : c + 1, k * TILE : (k + 1) * TILE] = col_sum[3, c * 16 + k : c * 16 + k + 1, :]
    net.finish()


def scatter(row_part, col_part):
    vmem = pl.BlockSpec(memory_space=pltpu.VMEM)
    block = lambda n: pltpu.VMEM((n, 48, TILE), F32)
    return pl.pallas_call(
        scatter_kernel,
        out_shape=jax.ShapeDtypeStruct((3, 2048), F32),
        in_specs=[vmem, vmem],
        out_specs=vmem,
        scratch_shapes=[
            block(16),
            block(16),
            block(4),
            block(8),
            pltpu.VMEM((2, 24, TILE), F32),
            block(2),
            block(2),
            block(4),
            pltpu.VMEM((48, TILE), F32),
            block(4),
            pltpu.SemaphoreType.DMA((SCATTER_COPIES,)),
            pltpu.SemaphoreType.DMA((SCATTER_COPIES,)),
        ],
        compiler_params=pltpu.CompilerParams(
            collective_id=1, has_side_effects=True, vmem_limit_bytes=16 * 1024 * 1024
        ),
        name="scatter_forces",
    )(row_part, col_part)


def shards(positions, type_ids, type_params, pair_tiles, pair_counts):
    row_data, col_data = gather(positions, type_ids.reshape(16, TILE))
    tiles = pair_tiles[0, 0].T
    row_part, col_part = forces_of(pair_counts, tiles, type_params, row_data, col_data)
    return scatter(row_part, col_part)


def solution(mesh):
    placed = (
        P(None, ("row", "col")),
        P(("row", "col")),
        P(),
        P("row", "col", None, None),
        P("row", "col"),
    )
    return jax.shard_map(
        shards, mesh=mesh, in_specs=placed, out_specs=P(None, ("row", "col")), check_vma=False
    )
```

```python
import math

import jax
import jax.numpy as jnp
from jax import lax
from jax.experimental import pallas as pl
from jax.experimental.pallas import tpu as pltpu
from jax.sharding import PartitionSpec as P

TILE = 128
NTYPES = 16
CUTOFF_SQ = 6.25
LOG2E = math.log2(math.e)
KAPPA = 2.0 / (CUTOFF_SQ * LOG2E)
UNROLL = 16
ROW_TILES = 512
COL_TILES = 128
F32 = jnp.float32
BF16 = jnp.bfloat16
MESH = pl.DeviceIdType.MESH


def pieces(value):
    high = value.astype(BF16).astype(F32)
    rest = value - high
    middle = rest.astype(BF16).astype(F32)
    return high, middle, rest, rest - middle


def distance_stack(value, order):
    high, middle, _, low = pieces(value)
    part = {"h": high, "m": middle, "l": low}
    return [jnp.concatenate([part[order[k]], part[order[k + 1]]], axis=0).astype(BF16) for k in (0, 2, 4)]


def moment_stack(value, upper):
    high, _, rest, low = pieces(value)
    return jnp.concatenate([jnp.where(upper, high, rest), jnp.where(upper, low, 0.0)], axis=0).astype(BF16)


def lanes_of(kinds):
    eye = lax.broadcasted_iota(jnp.int32, (NTYPES, NTYPES), 0) == lax.broadcasted_iota(jnp.int32, (NTYPES, NTYPES), 1)
    return jnp.sum(jnp.where(eye, kinds, 0.0), axis=1, keepdims=True)


def type_reader(params_ref):
    subf = lax.broadcasted_iota(jnp.int32, (8, TILE), 0).astype(F32)
    root = lanes_of(jnp.sqrt(params_ref[0:1, :]))
    root_a = jnp.broadcast_to(root[0:8], (8, TILE))
    root_b = jnp.broadcast_to(root[8:16], (8, TILE))

    def typed(kind):
        hit_a = subf == kind
        hit_b = subf + 8.0 == kind
        onehot = jnp.concatenate([jnp.where(hit_a, 1.0, 0.0), jnp.where(hit_b, 1.0, 0.0)], axis=0).astype(BF16)
        depth = jnp.sum(jnp.where(hit_a, root_a, 0.0) + jnp.where(hit_b, root_b, 0.0), axis=0, keepdims=True)
        return onehot, jnp.broadcast_to(depth, (8, TILE))

    return typed


def wide(ref, dev, comp, lane):
    return jnp.broadcast_to(ref[dev, comp : comp + 1, pl.ds(lane, TILE)], (8, TILE))


def spread(quad, x, y, z, last):
    return jnp.where(quad == 0, x, jnp.where(quad == 1, y, jnp.where(quad == 2, z, last)))


def column_preparer(params_ref, col_ref, feat, mom, cen, vel):
    sub = lax.broadcasted_iota(jnp.int32, (8, TILE), 0)
    quad = sub & 3
    width = params_ref[1:2, :]
    total = 0.5 * (lanes_of(width) + width)
    t_high, t_mid, _, t_low = pieces((CUTOFF_SQ * LOG2E) / (total * total))
    table48 = jnp.concatenate([t_high, t_mid, t_low], axis=0).astype(BF16)
    typed = type_reader(params_ref)
    zero_pack = jnp.zeros((16, TILE), BF16)

    def prepare(dev, k):
        b = dev * 16 + k
        x, y, z, kind = (wide(col_ref, dev, c, k * TILE) for c in range(4))
        here = spread(quad, x, y, z, 0.0)
        centre = jnp.sum(here, axis=1, keepdims=True) * (1.0 / TILE)
        cen[b] = jnp.broadcast_to(centre, (8, TILE))
        v = here - centre
        norm = jnp.sum(jnp.where(sub < 3, v * v, 0.0), axis=0, keepdims=True)
        onehot, depth = typed(kind)
        z8 = jnp.where(sub < 3, v * (2.0 / CUTOFF_SQ), jnp.where(sub == 3, 1.0, jnp.where(sub == 4, norm * (-1.0 / CUTOFF_SQ), 0.0)))
        second = jnp.dot(table48, onehot, preferred_element_type=F32).astype(BF16)
        stack = jnp.concatenate(distance_stack(z8, "hmlhmh") + [second, zero_pack, zero_pack], axis=0)
        feat[b] = stack.T
        mom[b] = moment_stack(jnp.where(quad == 3, 1.0, v) * depth, sub < 4)
        vel[b] = jnp.where(sub == 3, depth * KAPPA, v)

    def shard(dev):
        for k in range(16):
            prepare(dev, k)

    return shard


def force_kernel(count_ref, tiles_hbm, row_ref, feat, mom, cen, vel, params_ref, row_out, col_out, acc_row, acc_col, slope, mine, offset, scale, tiles_ref, load_sem):
    load_tiles = pltpu.make_async_copy(tiles_hbm, tiles_ref, load_sem)
    load_tiles.start()
    sub = lax.broadcasted_iota(jnp.int32, (8, TILE), 0)
    quad = sub & 3
    upper = sub < 4
    unit = jnp.where(sub == 4, 1.0, 0.0)
    typed = type_reader(params_ref)
    zero_pack = jnp.zeros((16, TILE), BF16)
    acc_row[...] = jnp.zeros_like(acc_row)
    acc_col[...] = jnp.zeros_like(acc_col)
    slope[...] = jnp.zeros_like(slope)
    mine[...] = jnp.zeros_like(mine)
    offset[...] = jnp.zeros_like(offset)
    scale[...] = jnp.zeros_like(scale)
    load_tiles.wait()
    count = count_ref[0, 0]

    def fold(out):
        first = out[0:8]
        return first + pltpu.roll(first, 4, 0) + out[8:16]

    zeros3 = [zero_pack] * 3
    zeros2 = [zero_pack] * 2

    def names(slot):
        live = (slot >= 0) & (slot < count)
        at = jnp.clip(slot, 0, count - 1)
        return live, tiles_ref[0, at], tiles_ref[1, at]

    def spread_out(slot, k):
        _, a, b = names(slot)
        owner = a // 16
        dev = (owner & 1) * 16 + (owner >> 1)
        lane = pl.multiple_of((a & 15) * TILE, TILE)
        x, y, z = (wide(row_ref, dev, c, lane) - jnp.broadcast_to(cen[b, c : c + 1, :], (8, TILE)) for c in range(3))
        kind = wide(row_ref, dev, 3, lane)
        onehot, depth = typed(kind)
        q = 1.0 - (x * x + y * y + z * z) * (1.0 / CUTOFF_SQ)
        xz = spread(quad, x, y, z, 1.0)
        z8 = jnp.where(sub < 3, xz, jnp.where(sub == 3, q, unit))
        near = jnp.concatenate(distance_stack(z8, "hhhmml") + zeros3 + zeros2, axis=0)
        kinds = jnp.concatenate(zeros3 + [onehot] * 3 + zeros2, axis=0)
        both = jnp.dot(feat[b], jnp.concatenate([near, kinds], axis=1), preferred_element_type=F32)
        c = jnp.maximum(both[:, :TILE], 0.0)
        decay = both[:, TILE:]
        u = c * decay
        g = (c * (u + 2.0 * LOG2E)) * jnp.exp2(u - decay)
        g_high = g.astype(BF16)
        g_low = (g - g_high.astype(F32)).astype(BF16)
        slope[k, 0:TILE, :] = g_high
        slope[k, TILE : 2 * TILE, :] = g_low
        mine[k] = moment_stack(xz * depth, upper)
        offset[k] = xz
        scale[k] = depth * KAPPA

    def gather_in(slot, k):
        live, a, b = names(slot)
        a_to = pl.multiple_of(jnp.where(live, a, ROW_TILES) * 8, 8)
        b_to = pl.multiple_of(jnp.where(live, b, COL_TILES) * 8, 8)
        sides = jnp.concatenate([mom[b], mine[k]], axis=0)
        g = slope[k]
        across = jnp.concatenate([g[:TILE].T, g[TILE:].T], axis=0)
        out = jnp.dot(
            jnp.concatenate([sides, sides], axis=1),
            jnp.concatenate([g, across], axis=1),
            preferred_element_type=F32,
        )
        to_i = fold(out[0:16, :TILE])
        to_j = fold(out[16:32, TILE:])
        weight = jnp.broadcast_to(to_i[3:4], (8, TILE))
        on_i = (offset[k] * weight - to_i) * scale[k]
        return a_to, b_to, on_i, to_j

    @pl.loop(0, pl.cdiv(count, UNROLL) + 1)
    def _(step):
        done = [gather_in((step - 1) * UNROLL + k, k) for k in range(UNROLL)]
        for k in range(UNROLL):
            spread_out(step * UNROLL + k, k)
        for a_to, b_to, on_i, to_j in done:
            acc_row[pl.ds(a_to, 8), :] += on_i
            acc_col[pl.ds(b_to, 8), :] += to_j

    @pl.loop(0, COL_TILES, step=4)
    def _(b0):
        for k in range(4):
            b = b0 + k
            at = pl.multiple_of(b * 8, 8)
            got = acc_col[pl.ds(at, 8), :]
            v = vel[b]
            weight = jnp.broadcast_to(got[3:4], (8, TILE))
            depth = jnp.broadcast_to(v[3:4], (8, TILE))
            acc_col[pl.ds(at, 8), :] = (v * weight - got) * depth

    for q in range(32):
        slot = (q & 1) * 16 + (q >> 1)
        for c in range(3):
            row_out[slot, c * 16 : c * 16 + 16, :] = acc_row[pl.ds(q * 128 + c, 16, stride=8), :]
    for p in range(8):
        for c in range(3):
            col_out[p, c * 16 : c * 16 + 16, :] = acc_col[pl.ds(p * 128 + c, 16, stride=8), :]


def forces_of(count, tiles, row_data, *columns):
    hbm = pl.BlockSpec(memory_space=pltpu.HBM)
    vmem = pl.BlockSpec(memory_space=pltpu.VMEM)
    return pl.pallas_call(
        force_kernel,
        out_shape=(jax.ShapeDtypeStruct((32, 48, TILE), F32), jax.ShapeDtypeStruct((8, 48, TILE), F32)),
        in_specs=[pl.BlockSpec(memory_space=pltpu.SMEM), hbm] + [vmem] * 6,
        out_specs=(vmem, vmem),
        scratch_shapes=[
            pltpu.VMEM(((ROW_TILES + 1) * 8, TILE), F32),
            pltpu.VMEM(((COL_TILES + 1) * 8, TILE), F32),
            pltpu.VMEM((UNROLL, 2 * TILE, TILE), BF16),
            pltpu.VMEM((UNROLL, 16, TILE), BF16),
            pltpu.VMEM((UNROLL, 8, TILE), F32),
            pltpu.VMEM((UNROLL, 8, TILE), F32),
            pltpu.SMEM((2, 384), jnp.int32),
            pltpu.SemaphoreType.DMA,
        ],
        compiler_params=pltpu.CompilerParams(vmem_limit_bytes=40 * 1024 * 1024),
        name="pair_forces",
    )(count, tiles, row_data, *columns)


def ring(v, d):
    return (v + d + 4) % 4


def place():
    p, q = lax.axis_index("row"), lax.axis_index("col")
    return p // 2, p % 2, q // 8, (q // 2) % 4, q % 2


def device(y, zl, zh, x, core):
    return (y * 2 + zl, zh * 8 + x * 2 + core)


STEPS = {"far": 2, "up": 1, "down": -1}


def neighbours(y, zl, zh, x, core):
    near = {"twin": device(y, zl, zh, x, 1 - core), "pal": device(y, 1 - zl, zh, x, core)}
    for name, d in STEPS.items():
        near["z_" + name] = device(y, zl, ring(zh, d), x, core)
        near["x_" + name] = device(y, zl, zh, ring(x, d), core)
        near["y_" + name] = device(ring(y, d), zl, zh, x, core)
    return near


def greet(near):
    barrier = pltpu.get_barrier_semaphore()
    for target in near.values():
        pl.semaphore_signal(barrier, inc=1, device_id=target, device_id_type=MESH)
    pl.semaphore_wait(barrier, len(near))


class Copies:
    def __init__(self, near, send_sem, recv_sem):
        self.near, self.send_sem, self.recv_sem = near, send_sem, recv_sem
        self.started = []

    def start(self, source, target, to):
        k = len(self.started)
        copy = pltpu.make_async_remote_copy(
            src_ref=source,
            dst_ref=target,
            send_sem=self.send_sem.at[k],
            recv_sem=self.recv_sem.at[k],
            device_id=self.near[to],
            device_id_type=MESH,
        )
        copy.start()
        self.started.append(copy)
        return copy

    def finish(self):
        for copy in self.started:
            copy.wait_send()


GATHER_COPIES = 38
SCATTER_COPIES = 23


def gather_kernel(pos_hbm, type_hbm, params_hbm, row_ref, col_ref, feat, mom, cen, vel, params_ref, pos_in, type_in, load_sem, send_sem, recv_sem):
    load_pos = pltpu.make_async_copy(pos_hbm, pos_in, load_sem.at[0])
    load_type = pltpu.make_async_copy(type_hbm, type_in, load_sem.at[1])
    load_params = pltpu.make_async_copy(params_hbm, params_ref, load_sem.at[2])
    load_pos.start()
    load_type.start()
    load_params.start()
    y, zl, zh, x, core = place()
    near = neighbours(y, zl, zh, x, core)
    at = lambda xx, zz: core * 16 + zz * 4 + xx
    col_at = lambda yy, ll: yy * 2 + ll
    mine, col_mine, col_pal = at(x, zh), col_at(y, zl), col_at(y, 1 - zl)
    load_pos.wait()
    load_type.wait()
    for ref, slot in ((row_ref, mine), (col_ref, col_mine)):
        ref[slot, 0:3, :] = pos_in[...]
        for k in range(16):
            ref[slot, 3:4, k * TILE : (k + 1) * TILE] = type_in[k : k + 1, :].astype(F32)
    greet(near)
    net = Copies(near, send_sem, recv_sem)

    def send(ref, slot, to):
        return net.start(ref.at[slot], ref.at[slot], to)

    along_z = {name: send(row_ref, mine, "z_" + name) for name in STEPS}
    along_x, along_y, twins = {}, {}, []
    pal = send(col_ref, col_mine, "pal")

    def pass_on(zz, key):
        along_x[key] = {name: send(row_ref, at(x, zz), "x_" + name) for name in STEPS}
        twins.append(send(row_ref, at(x, zz), "twin"))

    def pass_col(slot, key):
        along_y[key] = {name: send(col_ref, slot, "y_" + name) for name in STEPS}

    def hand_over(zz, key):
        for name in ("up", "down", "far"):
            along_x[key][name].wait_recv()
            twins.append(send(row_ref, at(ring(x, -STEPS[name]), zz), "twin"))

    pass_on(zh, "own")
    pass_col(col_mine, 0)
    load_params.wait()
    prepare = column_preparer(params_ref, col_ref, feat, mom, cen, vel)
    prepare(col_mine)
    pal.wait_recv()
    pass_col(col_pal, 1)
    for name in ("up", "down"):
        along_z[name].wait_recv()
        pass_on(ring(zh, -STEPS[name]), name)
    prepare(col_pal)
    hand_over(zh, "own")
    along_z["far"].wait_recv()
    pass_on(ring(zh, 2), "far")
    for name in ("up", "down"):
        along_y[0][name].wait_recv()
        prepare(col_at(ring(y, -STEPS[name]), zl))
    hand_over(ring(zh, -1), "up")
    hand_over(ring(zh, 1), "down")
    for name in ("up", "down"):
        along_y[1][name].wait_recv()
        prepare(col_at(ring(y, -STEPS[name]), 1 - zl))
    hand_over(ring(zh, 2), "far")
    for key, ll in ((0, zl), (1, 1 - zl)):
        along_y[key]["far"].wait_recv()
        prepare(col_at(ring(y, 2), ll))
    for copy in twins:
        copy.wait_recv()
    net.finish()


def in_hbm(array):
    return pltpu.with_memory_space_constraint(array, pltpu.HBM)


def gather(positions, kinds, params):
    hbm = pl.BlockSpec(memory_space=pltpu.HBM)
    vmem = pl.BlockSpec(memory_space=pltpu.VMEM)
    out = lambda *shape: jax.ShapeDtypeStruct(shape, F32)
    row_data, _, *columns = pl.pallas_call(
        gather_kernel,
        out_shape=(
            out(32, 4, 2048),
            out(8, 4, 2048),
            jax.ShapeDtypeStruct((COL_TILES, TILE, TILE), BF16),
            jax.ShapeDtypeStruct((COL_TILES, 16, TILE), BF16),
            out(COL_TILES, 8, TILE),
            out(COL_TILES, 8, TILE),
            out(2, NTYPES),
        ),
        in_specs=[hbm] * 3,
        out_specs=(vmem,) * 7,
        scratch_shapes=[
            pltpu.VMEM((3, 2048), F32),
            pltpu.VMEM((16, TILE), jnp.int32),
            pltpu.SemaphoreType.DMA((3,)),
            pltpu.SemaphoreType.DMA((GATHER_COPIES,)),
            pltpu.SemaphoreType.DMA((GATHER_COPIES,)),
        ],
        compiler_params=pltpu.CompilerParams(
            collective_id=0, has_side_effects=True, vmem_limit_bytes=24 * 1024 * 1024
        ),
        name="gather_atoms",
    )(*map(in_hbm, (positions, kinds, params)))
    return row_data, columns


def scatter_kernel(row_ref, col_ref, out_ref, from_twin, row_sum, x_in, z_out, z_in, y_in, col_sum, pal_in, send_sem, recv_sem):
    y, zl, zh, x, core = place()
    near = neighbours(y, zl, zh, x, core)
    greet(near)
    net = Copies(near, send_sem, recv_sem)
    offsets = (2, 1, -1, 0)
    order = ("far", "up", "down")

    twins = []
    for d in offsets:
        rows = ring(zh, d) * 4
        twins.append(net.start(row_ref.at[pl.ds((1 - core) * 16 + rows, 4)], from_twin.at[pl.ds(rows, 4)], "twin"))
    along_y = [net.start(col_ref.at[pl.ds(ring(y, STEPS[n]) * 2, 2)], y_in.at[k], "y_" + n) for k, n in enumerate(order)]

    along_x = []
    for i, d in enumerate(offsets):
        rows = ring(zh, d) * 4
        twins[i].wait_recv()
        row_sum[pl.ds(rows, 4)] = row_ref[pl.ds(core * 16 + rows, 4)] + from_twin[pl.ds(rows, 4)]
        along_x.append(
            [net.start(row_sum.at[rows + ring(x, STEPS[n])], x_in.at[i, k], "x_" + n) for k, n in enumerate(order)]
        )

    for copy in along_y:
        copy.wait_recv()
    here = y * 2
    col_sum[0] = col_ref[here + 1 - zl] + y_in[0, 1 - zl] + y_in[1, 1 - zl] + y_in[2, 1 - zl]
    pal = net.start(col_sum.at[0], pal_in, "pal")
    col_sum[1] = col_ref[here + zl] + y_in[0, zl] + y_in[1, zl] + y_in[2, zl]

    along_z = []
    for i, d in enumerate(offsets):
        for copy in along_x[i]:
            copy.wait_recv()
        total = row_sum[ring(zh, d) * 4 + x] + x_in[i, 0] + x_in[i, 1] + x_in[i, 2]
        if d:
            z_out[i] = total
            along_z.append(net.start(z_out.at[i], z_in.at[i], "z_" + order[i]))
        else:
            col_sum[1] = col_sum[1] + total
    pal.wait_recv()
    col_sum[1] = col_sum[1] + pal_in[...]
    for copy in along_z:
        copy.wait_recv()
    col_sum[1] = col_sum[1] + (z_in[0] + z_in[1] + z_in[2])
    for c in range(3):
        for k in range(16):
            out_ref[c : c + 1, k * TILE : (k + 1) * TILE] = col_sum[1, c * 16 + k : c * 16 + k + 1, :]
    net.finish()


def scatter(row_part, col_part):
    vmem = pl.BlockSpec(memory_space=pltpu.VMEM)
    block = lambda *n: pltpu.VMEM((*n, 48, TILE), F32)
    return pl.pallas_call(
        scatter_kernel,
        out_shape=jax.ShapeDtypeStruct((3, 2048), F32),
        in_specs=[vmem, vmem],
        out_specs=vmem,
        scratch_shapes=[
            block(16),
            block(16),
            block(4, 3),
            block(3),
            block(3),
            block(3, 2),
            block(2),
            block(),
            pltpu.SemaphoreType.DMA((SCATTER_COPIES,)),
            pltpu.SemaphoreType.DMA((SCATTER_COPIES,)),
        ],
        compiler_params=pltpu.CompilerParams(
            collective_id=1, has_side_effects=True, vmem_limit_bytes=16 * 1024 * 1024
        ),
        name="scatter_forces",
    )(row_part, col_part)


def shards(positions, type_ids, type_params, pair_tiles, pair_counts):
    row_data, columns = gather(positions, type_ids.reshape(16, TILE), type_params)
    tiles = pair_tiles[0, 0].T
    row_part, col_part = forces_of(pair_counts, in_hbm(tiles), row_data, *columns)
    return scatter(row_part, col_part)


def solution(mesh):
    placed = (
        P(None, ("row", "col")),
        P(("row", "col")),
        P(),
        P("row", "col", None, None),
        P("row", "col"),
    )
    return jax.shard_map(
        shards, mesh=mesh, in_specs=placed, out_specs=P(None, ("row", "col")), check_vma=False
    )
```

```python
import math

import jax
import jax.numpy as jnp
from jax import lax
from jax.experimental import pallas as pl
from jax.experimental.pallas import tpu as pltpu
from jax.sharding import PartitionSpec as P

TILE = 128
NTYPES = 16
CUTOFF_SQ = 6.25
LOG2E = math.log2(math.e)
KAPPA = 2.0 / (CUTOFF_SQ * LOG2E)
WIDTH_SCALE = 0.5 / math.sqrt(CUTOFF_SQ * LOG2E)
GROUP = 8
TURNS = 4
UNROLL = GROUP * TURNS
G2 = 2 * GROUP
U2 = GROUP
FIRST = 128
ROW_TILES = 512
COL_TILES = 128
F32 = jnp.float32
BF16 = jnp.bfloat16
MESH = pl.DeviceIdType.MESH


def pieces(value):
    high = value.astype(BF16).astype(F32)
    rest = value - high
    middle = rest.astype(BF16).astype(F32)
    return high, middle, rest, rest - middle


def distance_stack(value, order):
    high, middle, _, low = pieces(value)
    part = {"h": high, "m": middle, "l": low}
    return [jnp.concatenate([part[order[k]], part[order[k + 1]]], axis=0).astype(BF16) for k in (0, 2, 4)]


def moment_stack(value, upper):
    high = value.astype(BF16).astype(F32)
    return jnp.where(upper, high, value - high)


def look_up(table, kind):
    both = jnp.take_along_axis(table, kind.astype(jnp.int32), axis=1)
    return jnp.broadcast_to(both[0:1], (8, TILE)), jnp.broadcast_to(both[4:5], (8, TILE))


def wide(ref, dev, comp, lane):
    return jnp.broadcast_to(ref[dev, comp : comp + 1, pl.ds(lane, TILE)], (8, TILE))


def spread(quad, x, y, z, last):
    return jnp.where(quad == 0, x, jnp.where(quad == 1, y, jnp.where(quad == 2, z, last)))


def column_preparer(table, col_ref, feat, mom, cen, vel, wid):
    sub = lax.broadcasted_iota(jnp.int32, (8, TILE), 0)
    quad = sub & 3
    zero8 = jnp.zeros((8, TILE), F32)
    types = table[...]
    zeros = jnp.zeros((64, TILE), BF16)
    row = lax.broadcasted_iota(jnp.int32, (TILE, TILE), 0)
    pick = jnp.where((row >= 48) & (row < 51), 1.0, 0.0).astype(BF16)

    def prepare(dev, k):
        b = dev * 16 + k
        x, y, z, kind = (wide(col_ref, dev, c, k * TILE) for c in range(4))
        here = spread(quad, x, y, z, 0.0)
        centre = jnp.sum(here, axis=1, keepdims=True) * (1.0 / TILE)
        cen[b] = jnp.broadcast_to(centre, (8, TILE))
        v = here - centre
        norm = jnp.sum(jnp.where(sub < 3, v * v, 0.0), axis=0, keepdims=True)
        depth, width = look_up(types, kind)
        z8 = jnp.where(sub < 3, v * (2.0 / CUTOFF_SQ), jnp.where(sub == 3, 1.0, jnp.where(sub == 4, norm * (-1.0 / CUTOFF_SQ), 0.0)))
        high, middle, _, low = pieces(width)
        widths = jnp.where(sub == 0, high, jnp.where(sub == 1, middle, jnp.where(sub == 2, low, 0.0)))
        widths = jnp.concatenate([widths, zero8], axis=0).astype(BF16)
        turned = jnp.concatenate(distance_stack(z8, "hmlhmh") + [widths, zeros], axis=0).T
        feat[b] = turned
        wid[b] = jnp.dot(turned, pick, preferred_element_type=F32)
        mom[b] = moment_stack(jnp.where(quad == 3, 1.0, v) * depth, sub < 4)
        vel[b] = jnp.where(sub == 3, depth * KAPPA, v)

    def shard(dev):
        for k in range(16):
            prepare(dev, k)

    return shard


def force_kernel(count_ref, tiles_hbm, row_ref, feat, mom, cen, vel, wid, table, row_out, col_out, acc_row, acc_col, slope, mine, offset, scale, span, reach, tiles_ref, load_sem):
    load_tiles = pltpu.make_async_copy(tiles_hbm, tiles_ref.at[:, pl.ds(FIRST, 384)], load_sem)
    load_tiles.start()
    sub = lax.broadcasted_iota(jnp.int32, (8, TILE), 0)
    quad = sub & 3
    upper = sub < 4
    unit = jnp.where(sub == 4, 1.0, 0.0)
    types = table[...]
    zeros80 = jnp.zeros((80, TILE), BF16)
    zeros128 = jnp.zeros((TILE, TILE), BF16)
    acc_row[...] = jnp.zeros_like(acc_row)
    acc_col[...] = jnp.zeros_like(acc_col)
    load_tiles.wait()
    count = count_ref[0, 0]
    for k in range(-2 * GROUP, 6 * GROUP):
        at = FIRST + k + (0 if k < 0 else count)
        tiles_ref[0, at] = ROW_TILES
        tiles_ref[1, at] = COL_TILES

    def fold(out):
        return out + pltpu.roll(out, 4, 0)

    def nearness(slot, k):
        a, b = tiles_ref[0, slot] & (ROW_TILES - 1), tiles_ref[1, slot] & (COL_TILES - 1)
        dev = (a & 16) + (a >> 5)
        lane = pl.multiple_of((a & 15) * TILE, TILE)
        x, y, z = (wide(row_ref, dev, c, lane) - jnp.broadcast_to(cen[b, c : c + 1, :], (8, TILE)) for c in range(3))
        kind = wide(row_ref, dev, 3, lane)
        depth, width = look_up(types, kind)
        q = 1.0 - (x * x + y * y + z * z) * (1.0 / CUTOFF_SQ)
        xz = spread(quad, x, y, z, 1.0)
        z8 = jnp.where(sub < 3, xz, jnp.where(sub == 3, q, unit))
        mine[k][...] = moment_stack(xz * depth, upper)
        offset[k][...] = xz
        scale[k][...] = depth * KAPPA
        span[k][...] = width
        return b, jnp.concatenate(distance_stack(z8, "hhhmml") + [zeros80], axis=0)

    def measure(slot, k):
        sides = [nearness(slot + n, k + n) for n in range(2)]
        feats = jnp.concatenate([feat[b] for b, _ in sides], axis=1)
        first, second = (near for _, near in sides)
        weights = jnp.concatenate(
            [jnp.concatenate([first, zeros128], axis=1), jnp.concatenate([zeros128, second], axis=1)], axis=0
        )
        reach[k // 2 % U2][...] = jnp.dot(feats, weights, preferred_element_type=F32)

    def spread_out(slot, k):
        b = tiles_ref[1, slot] & (COL_TILES - 1)
        half = (k % 2) * TILE
        c = jnp.maximum(reach[k // 2 % U2][:, half : half + TILE], 0.0)
        spans = wid[b].reshape(16, 8, TILE) + span[k][...][None]
        inverse = pl.reciprocal(spans.reshape(TILE, TILE), approx=True)
        decay = inverse * inverse
        u = c * decay
        g = (c * (u + 2.0 * LOG2E)) * jnp.exp2(u - decay)
        g_high = g.astype(BF16)
        g_low = (g - g_high.astype(F32)).astype(BF16)
        slope[k % G2][0:TILE, :] = g_high
        slope[k % G2][TILE : 2 * TILE, :] = g_low

    def gather_in(slot, k):
        a, b = tiles_ref[0, slot], tiles_ref[1, slot]
        a_to, b_to = pl.multiple_of(a * 8, 8), pl.multiple_of(b * 8, 8)
        sides = jnp.concatenate([mom[b & (COL_TILES - 1)], mine[k][...]], axis=0).astype(BF16)
        g = slope[k % G2][...]
        across = jnp.concatenate([g[:TILE].T, g[TILE:].T], axis=0)
        out = jnp.dot(
            jnp.concatenate([sides, sides], axis=1),
            jnp.concatenate([g, across], axis=1),
            preferred_element_type=F32,
        )
        to_i = fold(out[0:8, :TILE])
        to_j = fold(out[8:16, TILE:])
        weight = jnp.broadcast_to(to_i[3:4], (8, TILE))
        on_i = (offset[k][...] * weight - to_i) * scale[k][...]
        return a_to, b_to, on_i, to_j

    def collect(slot, k):
        a_to, b_to, on_i, to_j = gather_in(slot, k)
        acc_row[pl.ds(a_to, 8), :] += on_i
        acc_col[pl.ds(b_to, 8), :] += to_j

    @pl.loop(0, pl.cdiv(pl.cdiv(count, GROUP) + 2, TURNS))
    def _(turn):
        base = FIRST + turn * (TURNS * GROUP)
        for h in range(TURNS):
            for n in range(GROUP):
                collect(base + (h - 2) * GROUP + n, (h - 2) % TURNS * GROUP + n)
                spread_out(base + (h - 1) * GROUP + n, (h - 1) % TURNS * GROUP + n)
                if n % 2:
                    measure(base + h * GROUP + n - 1, h * GROUP + n - 1)

    @pl.loop(0, COL_TILES, step=4)
    def _(b0):
        for k in range(4):
            b = b0 + k
            at = pl.multiple_of(b * 8, 8)
            got = acc_col[pl.ds(at, 8), :]
            v = vel[b]
            weight = jnp.broadcast_to(got[3:4], (8, TILE))
            depth = jnp.broadcast_to(v[3:4], (8, TILE))
            acc_col[pl.ds(at, 8), :] = (v * weight - got) * depth

    for q in range(32):
        slot = (q & 1) * 16 + (q >> 1)
        for c in range(3):
            row_out[slot, c * 16 : c * 16 + 16, :] = acc_row[pl.ds(q * 128 + c, 16, stride=8), :]
    for p in range(8):
        for c in range(3):
            col_out[p, c * 16 : c * 16 + 16, :] = acc_col[pl.ds(p * 128 + c, 16, stride=8), :]


def forces_of(count, tiles, row_data, *columns):
    hbm = pl.BlockSpec(memory_space=pltpu.HBM)
    vmem = pl.BlockSpec(memory_space=pltpu.VMEM)
    return pl.pallas_call(
        force_kernel,
        out_shape=(jax.ShapeDtypeStruct((32, 48, TILE), F32), jax.ShapeDtypeStruct((8, 48, TILE), F32)),
        in_specs=[pl.BlockSpec(memory_space=pltpu.SMEM), hbm] + [vmem] * 7,
        out_specs=(vmem, vmem),
        scratch_shapes=[
            pltpu.VMEM(((ROW_TILES + 1) * 8, TILE), F32),
            pltpu.VMEM(((COL_TILES + 1) * 8, TILE), F32),
            [pltpu.VMEM((2 * TILE, TILE), BF16)] * G2,
            [pltpu.VMEM((8, TILE), F32)] * UNROLL,
            [pltpu.VMEM((8, TILE), F32)] * UNROLL,
            [pltpu.VMEM((8, TILE), F32)] * UNROLL,
            [pltpu.VMEM((8, TILE), F32)] * UNROLL,
            [pltpu.VMEM((TILE, 2 * TILE), F32)] * U2,
            pltpu.SMEM((2, FIRST + 384 + 128), jnp.int32),
            pltpu.SemaphoreType.DMA,
        ],
        compiler_params=pltpu.CompilerParams(vmem_limit_bytes=40 * 1024 * 1024),
        name="pair_forces",
    )(count, tiles, row_data, *columns)


def ring(v, d):
    return (v + d + 4) % 4


def place():
    p, q = lax.axis_index("row"), lax.axis_index("col")
    return p // 2, p % 2, q // 8, (q // 2) % 4, q % 2


def device(y, zl, zh, x, core):
    return (y * 2 + zl, zh * 8 + x * 2 + core)


STEPS = {"far": 2, "up": 1, "down": -1}


def neighbours(y, zl, zh, x, core):
    near = {"twin": device(y, zl, zh, x, 1 - core), "pal": device(y, 1 - zl, zh, x, core)}
    for name, d in STEPS.items():
        near["z_" + name] = device(y, zl, ring(zh, d), x, core)
        near["x_" + name] = device(y, zl, zh, ring(x, d), core)
        near["y_" + name] = device(ring(y, d), zl, zh, x, core)
    return near


def greet(near):
    for target in near.values():
        pl.semaphore_signal(pltpu.get_barrier_semaphore(), inc=1, device_id=target, device_id_type=MESH)


def await_greetings(near):
    pl.semaphore_wait(pltpu.get_barrier_semaphore(), len(near))


class Copies:
    def __init__(self, near, send_sem, recv_sem):
        self.near, self.send_sem, self.recv_sem = near, send_sem, recv_sem
        self.started = []

    def start(self, source, target, to):
        k = len(self.started)
        copy = pltpu.make_async_remote_copy(
            src_ref=source,
            dst_ref=target,
            send_sem=self.send_sem.at[k],
            recv_sem=self.recv_sem.at[k],
            device_id=self.near[to],
            device_id_type=MESH,
        )
        copy.start()
        self.started.append(copy)
        return copy

    def finish(self):
        for copy in self.started:
            copy.wait_send()


GATHER_COPIES = 38
SCATTER_COPIES = 23


def gather_kernel(pos_hbm, type_hbm, params_hbm, row_ref, feat, mom, cen, vel, wid, table, col_ref, params_ref, pos_in, type_in, load_sem, send_sem, recv_sem):
    load_pos = pltpu.make_async_copy(pos_hbm, pos_in, load_sem.at[0])
    load_type = pltpu.make_async_copy(type_hbm, type_in, load_sem.at[1])
    load_params = pltpu.make_async_copy(params_hbm, params_ref, load_sem.at[2])
    load_pos.start()
    load_type.start()
    load_params.start()
    y, zl, zh, x, core = place()
    near = neighbours(y, zl, zh, x, core)
    greet(near)
    at = lambda xx, zz: core * 16 + zz * 4 + xx
    col_at = lambda yy, ll: yy * 2 + ll
    mine, col_mine, col_pal = at(x, zh), col_at(y, zl), col_at(y, 1 - zl)
    load_pos.wait()
    load_type.wait()
    for ref, slot in ((row_ref, mine), (col_ref, col_mine)):
        ref[slot, 0:3, :] = pos_in[...]
        for k in range(16):
            ref[slot, 3:4, k * TILE : (k + 1) * TILE] = type_in[k : k + 1, :].astype(F32)
    await_greetings(near)
    net = Copies(near, send_sem, recv_sem)

    def send(ref, slot, to):
        return net.start(ref.at[slot], ref.at[slot], to)

    along_z = {name: send(row_ref, mine, "z_" + name) for name in STEPS}
    along_x, along_y, twins = {}, {}, []
    pal = send(col_ref, col_mine, "pal")

    def pass_on(zz, key):
        along_x[key] = {name: send(row_ref, at(x, zz), "x_" + name) for name in STEPS}
        twins.append(send(row_ref, at(x, zz), "twin"))

    def pass_col(slot, key):
        along_y[key] = {name: send(col_ref, slot, "y_" + name) for name in STEPS}

    def hand_over(zz, key):
        for name in ("up", "down", "far"):
            along_x[key][name].wait_recv()
            twins.append(send(row_ref, at(ring(x, -STEPS[name]), zz), "twin"))

    pass_on(zh, "own")
    pass_col(col_mine, 0)
    load_params.wait()
    table[...] = jnp.zeros_like(table)
    for k in range(4):
        table[k : k + 1, 0:NTYPES] = jnp.sqrt(params_ref[0:1, :])
        table[k + 4 : k + 5, 0:NTYPES] = params_ref[1:2, :] * WIDTH_SCALE
    prepare = column_preparer(table, col_ref, feat, mom, cen, vel, wid)
    prepare(col_mine)
    pal.wait_recv()
    pass_col(col_pal, 1)
    for name in ("up", "down"):
        along_z[name].wait_recv()
        pass_on(ring(zh, -STEPS[name]), name)
    prepare(col_pal)
    hand_over(zh, "own")
    along_z["far"].wait_recv()
    pass_on(ring(zh, 2), "far")
    for name in ("up", "down"):
        along_y[0][name].wait_recv()
        prepare(col_at(ring(y, -STEPS[name]), zl))
    hand_over(ring(zh, -1), "up")
    hand_over(ring(zh, 1), "down")
    for name in ("up", "down"):
        along_y[1][name].wait_recv()
        prepare(col_at(ring(y, -STEPS[name]), 1 - zl))
    hand_over(ring(zh, 2), "far")
    for key, ll in ((0, zl), (1, 1 - zl)):
        along_y[key]["far"].wait_recv()
        prepare(col_at(ring(y, 2), ll))
    for copy in twins:
        copy.wait_recv()
    net.finish()


def in_hbm(array):
    return pltpu.with_memory_space_constraint(array, pltpu.HBM)


def gather(positions, kinds, params):
    hbm = pl.BlockSpec(memory_space=pltpu.HBM)
    vmem = pl.BlockSpec(memory_space=pltpu.VMEM)
    out = lambda *shape: jax.ShapeDtypeStruct(shape, F32)
    row_data, *columns = pl.pallas_call(
        gather_kernel,
        out_shape=(
            out(32, 4, 2048),
            jax.ShapeDtypeStruct((COL_TILES, TILE, TILE), BF16),
            out(COL_TILES, 8, TILE),
            out(COL_TILES, 8, TILE),
            out(COL_TILES, 8, TILE),
            out(COL_TILES, TILE, TILE),
            out(8, TILE),
        ),
        in_specs=[hbm] * 3,
        out_specs=(vmem,) * 7,
        scratch_shapes=[
            pltpu.VMEM((8, 4, 2048), F32),
            pltpu.VMEM((2, NTYPES), F32),
            pltpu.VMEM((3, 2048), F32),
            pltpu.VMEM((16, TILE), jnp.int32),
            pltpu.SemaphoreType.DMA((3,)),
            pltpu.SemaphoreType.DMA((GATHER_COPIES,)),
            pltpu.SemaphoreType.DMA((GATHER_COPIES,)),
        ],
        compiler_params=pltpu.CompilerParams(
            collective_id=0, has_side_effects=True, vmem_limit_bytes=32 * 1024 * 1024
        ),
        name="gather_atoms",
    )(*map(in_hbm, (positions, kinds, params)))
    return row_data, columns


def scatter_kernel(row_ref, col_ref, out_ref, from_twin, row_sum, x_in, z_out, z_in, y_in, col_sum, pal_in, send_sem, recv_sem):
    y, zl, zh, x, core = place()
    near = neighbours(y, zl, zh, x, core)
    greet(near)
    await_greetings(near)
    net = Copies(near, send_sem, recv_sem)
    offsets = (2, 1, -1, 0)
    order = ("far", "up", "down")

    twins = []
    for d in offsets:
        rows = ring(zh, d) * 4
        twins.append(net.start(row_ref.at[pl.ds((1 - core) * 16 + rows, 4)], from_twin.at[pl.ds(rows, 4)], "twin"))
    along_y = [net.start(col_ref.at[pl.ds(ring(y, STEPS[n]) * 2, 2)], y_in.at[k], "y_" + n) for k, n in enumerate(order)]

    along_x = []
    for i, d in enumerate(offsets):
        rows = ring(zh, d) * 4
        twins[i].wait_recv()
        row_sum[pl.ds(rows, 4)] = row_ref[pl.ds(core * 16 + rows, 4)] + from_twin[pl.ds(rows, 4)]
        along_x.append(
            [net.start(row_sum.at[rows + ring(x, STEPS[n])], x_in.at[i, k], "x_" + n) for k, n in enumerate(order)]
        )

    for copy in along_y:
        copy.wait_recv()
    here = y * 2
    col_sum[0] = col_ref[here + 1 - zl] + y_in[0, 1 - zl] + y_in[1, 1 - zl] + y_in[2, 1 - zl]
    pal = net.start(col_sum.at[0], pal_in, "pal")
    col_sum[1] = col_ref[here + zl] + y_in[0, zl] + y_in[1, zl] + y_in[2, zl]

    along_z = []
    for i, d in enumerate(offsets):
        for copy in along_x[i]:
            copy.wait_recv()
        total = row_sum[ring(zh, d) * 4 + x] + x_in[i, 0] + x_in[i, 1] + x_in[i, 2]
        if d:
            z_out[i] = total
            along_z.append(net.start(z_out.at[i], z_in.at[i], "z_" + order[i]))
        else:
            col_sum[1] = col_sum[1] + total
    pal.wait_recv()
    col_sum[1] = col_sum[1] + pal_in[...]
    for copy in along_z:
        copy.wait_recv()
    col_sum[1] = col_sum[1] + (z_in[0] + z_in[1] + z_in[2])
    for c in range(3):
        for k in range(16):
            out_ref[c : c + 1, k * TILE : (k + 1) * TILE] = col_sum[1, c * 16 + k : c * 16 + k + 1, :]
    net.finish()


def scatter(row_part, col_part):
    vmem = pl.BlockSpec(memory_space=pltpu.VMEM)
    block = lambda *n: pltpu.VMEM((*n, 48, TILE), F32)
    return pl.pallas_call(
        scatter_kernel,
        out_shape=jax.ShapeDtypeStruct((3, 2048), F32),
        in_specs=[vmem, vmem],
        out_specs=vmem,
        scratch_shapes=[
            block(16),
            block(16),
            block(4, 3),
            block(3),
            block(3),
            block(3, 2),
            block(2),
            block(),
            pltpu.SemaphoreType.DMA((SCATTER_COPIES,)),
            pltpu.SemaphoreType.DMA((SCATTER_COPIES,)),
        ],
        compiler_params=pltpu.CompilerParams(
            collective_id=1, has_side_effects=True, vmem_limit_bytes=16 * 1024 * 1024
        ),
        name="scatter_forces",
    )(row_part, col_part)


def shards(positions, type_ids, type_params, pair_tiles, pair_counts):
    row_data, columns = gather(positions, type_ids.reshape(16, TILE), type_params)
    tiles = pair_tiles[0, 0].T
    row_part, col_part = forces_of(pair_counts, in_hbm(tiles), row_data, *columns)
    return scatter(row_part, col_part)


def solution(mesh):
    placed = (
        P(None, ("row", "col")),
        P(("row", "col")),
        P(),
        P("row", "col", None, None),
        P("row", "col"),
    )
    return jax.shard_map(
        shards, mesh=mesh, in_specs=placed, out_specs=P(None, ("row", "col")), check_vma=False
    )
```

```python
import math

import jax
import jax.numpy as jnp
from jax import lax
from jax.experimental import pallas as pl
from jax.experimental.pallas import tpu as pltpu
from jax.sharding import PartitionSpec as P

TILE = 128
NTYPES = 16
CUTOFF_SQ = 6.25
LOG2E = math.log2(math.e)
KAPPA = 2.0 / (CUTOFF_SQ * LOG2E)
WIDTH_SCALE = 0.5 / math.sqrt(CUTOFF_SQ * LOG2E)
GROUP = 8
TURNS = 4
UNROLL = GROUP * TURNS
G2 = 2 * GROUP
U2 = GROUP
FIRST = 128
ROW_TILES = 512
COL_TILES = 128
F32 = jnp.float32
BF16 = jnp.bfloat16
MESH = pl.DeviceIdType.MESH


def pieces(value):
    high = value.astype(BF16).astype(F32)
    rest = value - high
    middle = rest.astype(BF16).astype(F32)
    return high, middle, rest, rest - middle


def distance_stack(value, order):
    high, middle, _, low = pieces(value)
    part = {"h": high, "m": middle, "l": low}
    return [jnp.concatenate([part[order[k]], part[order[k + 1]]], axis=0).astype(BF16) for k in (0, 2, 4)]


def moment_stack(value, upper):
    high = value.astype(BF16).astype(F32)
    return jnp.where(upper, high, value - high)


def look_up(table, kind):
    both = jnp.take_along_axis(table, kind.astype(jnp.int32), axis=1)
    return jnp.broadcast_to(both[0:1], (8, TILE)), jnp.broadcast_to(both[4:5], (8, TILE))


def wide(ref, dev, comp, lane):
    return jnp.broadcast_to(ref[dev, comp : comp + 1, pl.ds(lane, TILE)], (8, TILE))


def spread(quad, x, y, z, last):
    return jnp.where(quad == 0, x, jnp.where(quad == 1, y, jnp.where(quad == 2, z, last)))


def column_preparer(table, col_ref, feat, mom, cen, vel, wid):
    sub = lax.broadcasted_iota(jnp.int32, (8, TILE), 0)
    quad = sub & 3
    zero8 = jnp.zeros((8, TILE), F32)
    types = table[...]
    zeros = jnp.zeros((64, TILE), BF16)
    row = lax.broadcasted_iota(jnp.int32, (TILE, TILE), 0)
    pick = jnp.where((row >= 48) & (row < 51), 1.0, 0.0).astype(BF16)

    def prepare(dev, k):
        b = dev * 16 + k
        x, y, z, kind = (wide(col_ref, dev, c, k * TILE) for c in range(4))
        here = spread(quad, x, y, z, 0.0)
        centre = jnp.sum(here, axis=1, keepdims=True) * (1.0 / TILE)
        cen[b] = jnp.broadcast_to(centre, (8, TILE))
        v = here - centre
        norm = jnp.sum(jnp.where(sub < 3, v * v, 0.0), axis=0, keepdims=True)
        depth, width = look_up(types, kind)
        z8 = jnp.where(sub < 3, v * (2.0 / CUTOFF_SQ), jnp.where(sub == 3, 1.0, jnp.where(sub == 4, norm * (-1.0 / CUTOFF_SQ), 0.0)))
        high, middle, _, low = pieces(width)
        widths = jnp.where(sub == 0, high, jnp.where(sub == 1, middle, jnp.where(sub == 2, low, 0.0)))
        widths = jnp.concatenate([widths, zero8], axis=0).astype(BF16)
        turned = jnp.concatenate(distance_stack(z8, "hmlhmh") + [widths, zeros], axis=0).T
        feat[b] = turned
        wid[b] = jnp.dot(turned, pick, preferred_element_type=F32)
        mom[b] = moment_stack(jnp.where(quad == 3, 1.0, v) * depth, sub < 4)
        vel[b] = jnp.where(sub == 3, depth * KAPPA, v)

    def shard(dev):
        for k in range(16):
            prepare(dev, k)

    return shard


def force_kernel(count_ref, tiles_hbm, row_ref, feat, mom, cen, vel, wid, table, row_out, col_out, acc_row, acc_col, slope, mine, offset, scale, span, reach, tiles_ref, load_sem):
    load_tiles = pltpu.make_async_copy(tiles_hbm, tiles_ref.at[:, pl.ds(FIRST, 384)], load_sem)
    load_tiles.start()
    sub = lax.broadcasted_iota(jnp.int32, (8, TILE), 0)
    quad = sub & 3
    upper = sub < 4
    unit = jnp.where(sub == 4, 1.0, 0.0)
    types = table[...]
    zeros80 = jnp.zeros((80, TILE), BF16)
    zeros128 = jnp.zeros((TILE, TILE), BF16)
    acc_row[...] = jnp.zeros_like(acc_row)
    acc_col[...] = jnp.zeros_like(acc_col)
    load_tiles.wait()
    count = count_ref[0, 0]
    for k in range(-2 * GROUP, 6 * GROUP):
        at = FIRST + k + (0 if k < 0 else count)
        tiles_ref[0, at] = ROW_TILES
        tiles_ref[1, at] = COL_TILES

    def fold(out):
        return out + pltpu.roll(out, 4, 0)

    def nearness(slot, k):
        a, b = tiles_ref[0, slot] & (ROW_TILES - 1), tiles_ref[1, slot] & (COL_TILES - 1)
        dev = (a & 16) + (a >> 5)
        lane = pl.multiple_of((a & 15) * TILE, TILE)
        x, y, z = (wide(row_ref, dev, c, lane) - jnp.broadcast_to(cen[b, c : c + 1, :], (8, TILE)) for c in range(3))
        kind = wide(row_ref, dev, 3, lane)
        depth, width = look_up(types, kind)
        q = 1.0 - (x * x + y * y + z * z) * (1.0 / CUTOFF_SQ)
        xz = spread(quad, x, y, z, 1.0)
        z8 = jnp.where(sub < 3, xz, jnp.where(sub == 3, q, unit))
        mine[k][...] = moment_stack(xz * depth, upper)
        offset[k][...] = xz
        scale[k][...] = depth * KAPPA
        span[k][...] = width
        return b, jnp.concatenate(distance_stack(z8, "hhhmml") + [zeros80], axis=0)

    def measure(slot, k):
        sides = [nearness(slot + n, k + n) for n in range(2)]
        feats = jnp.concatenate([feat[b] for b, _ in sides], axis=1)
        first, second = (near for _, near in sides)
        weights = jnp.concatenate(
            [jnp.concatenate([first, zeros128], axis=1), jnp.concatenate([zeros128, second], axis=1)], axis=0
        )
        reach[k // 2 % U2][...] = jnp.dot(feats, weights, preferred_element_type=F32)

    def spread_out(slot, k):
        b = tiles_ref[1, slot] & (COL_TILES - 1)
        half = (k % 2) * TILE
        c = jnp.maximum(reach[k // 2 % U2][:, half : half + TILE], 0.0)
        spans = wid[b].reshape(16, 8, TILE) + span[k][...][None]
        inverse = pl.reciprocal(spans.reshape(TILE, TILE), approx=True)
        decay = inverse * inverse
        u = c * decay
        g = (c * (u + 2.0 * LOG2E)) * jnp.exp2(u - decay)
        g_high = g.astype(BF16)
        g_low = (g - g_high.astype(F32)).astype(BF16)
        slope[k % G2][0:TILE, :] = g_high
        slope[k % G2][TILE : 2 * TILE, :] = g_low

    def gather_in(slot, k):
        a, b = tiles_ref[0, slot], tiles_ref[1, slot]
        a_to, b_to = pl.multiple_of(a * 8, 8), pl.multiple_of(b * 8, 8)
        sides = jnp.concatenate([mom[b & (COL_TILES - 1)], mine[k][...]], axis=0).astype(BF16)
        g = slope[k % G2][...]
        across = jnp.concatenate([g[:TILE].T, g[TILE:].T], axis=0)
        out = jnp.dot(
            jnp.concatenate([sides, sides], axis=1),
            jnp.concatenate([g, across], axis=1),
            preferred_element_type=F32,
        )
        to_i = fold(out[0:8, :TILE])
        to_j = fold(out[8:16, TILE:])
        weight = jnp.broadcast_to(to_i[3:4], (8, TILE))
        on_i = (offset[k][...] * weight - to_i) * scale[k][...]
        return a_to, b_to, on_i, to_j

    def collect(slot, k):
        a_to, b_to, on_i, to_j = gather_in(slot, k)
        acc_row[pl.ds(a_to, 8), :] += on_i
        acc_col[pl.ds(b_to, 8), :] += to_j

    @pl.loop(0, pl.cdiv(pl.cdiv(count, GROUP) + 2, TURNS))
    def _(turn):
        base = FIRST + turn * (TURNS * GROUP)
        for h in range(TURNS):
            for n in range(GROUP):
                collect(base + (h - 2) * GROUP + n, (h - 2) % TURNS * GROUP + n)
                spread_out(base + (h - 1) * GROUP + n, (h - 1) % TURNS * GROUP + n)
                if n % 2:
                    measure(base + h * GROUP + n - 1, h * GROUP + n - 1)

    @pl.loop(0, COL_TILES, step=4)
    def _(b0):
        for k in range(4):
            b = b0 + k
            at = pl.multiple_of(b * 8, 8)
            got = acc_col[pl.ds(at, 8), :]
            v = vel[b]
            weight = jnp.broadcast_to(got[3:4], (8, TILE))
            depth = jnp.broadcast_to(v[3:4], (8, TILE))
            acc_col[pl.ds(at, 8), :] = (v * weight - got) * depth

    for q in range(32):
        slot = (q & 1) * 16 + (q >> 1)
        for c in range(3):
            row_out[slot, c * 16 : c * 16 + 16, :] = acc_row[pl.ds(q * 128 + c, 16, stride=8), :]
    for p in range(8):
        for c in range(3):
            col_out[p, c * 16 : c * 16 + 16, :] = acc_col[pl.ds(p * 128 + c, 16, stride=8), :]


def forces_of(count, tiles, row_data, *columns):
    hbm = pl.BlockSpec(memory_space=pltpu.HBM)
    vmem = pl.BlockSpec(memory_space=pltpu.VMEM)
    return pl.pallas_call(
        force_kernel,
        out_shape=(jax.ShapeDtypeStruct((32, 48, TILE), F32), jax.ShapeDtypeStruct((8, 48, TILE), F32)),
        in_specs=[pl.BlockSpec(memory_space=pltpu.SMEM), hbm] + [vmem] * 7,
        out_specs=(vmem, vmem),
        scratch_shapes=[
            pltpu.VMEM(((ROW_TILES + 1) * 8, TILE), F32),
            pltpu.VMEM(((COL_TILES + 1) * 8, TILE), F32),
            [pltpu.VMEM((2 * TILE, TILE), BF16)] * G2,
            [pltpu.VMEM((8, TILE), F32)] * UNROLL,
            [pltpu.VMEM((8, TILE), F32)] * UNROLL,
            [pltpu.VMEM((8, TILE), F32)] * UNROLL,
            [pltpu.VMEM((8, TILE), F32)] * UNROLL,
            [pltpu.VMEM((TILE, 2 * TILE), F32)] * U2,
            pltpu.SMEM((2, FIRST + 384 + 128), jnp.int32),
            pltpu.SemaphoreType.DMA,
        ],
        compiler_params=pltpu.CompilerParams(vmem_limit_bytes=26 * 1024 * 1024),
        name="pair_forces",
    )(count, tiles, row_data, *columns)


def ring(v, d):
    return (v + d + 4) % 4


def place():
    p, q = lax.axis_index("row"), lax.axis_index("col")
    return p // 2, p % 2, q // 8, (q // 2) % 4, q % 2


def device(y, zl, zh, x, core):
    return (y * 2 + zl, zh * 8 + x * 2 + core)


STEPS = {"far": 2, "up": 1, "down": -1}


def neighbours(y, zl, zh, x, core):
    near = {"twin": device(y, zl, zh, x, 1 - core), "pal": device(y, 1 - zl, zh, x, core)}
    for name, d in STEPS.items():
        near["z_" + name] = device(y, zl, ring(zh, d), x, core)
        near["x_" + name] = device(y, zl, zh, ring(x, d), core)
        near["y_" + name] = device(ring(y, d), zl, zh, x, core)
    return near


def greet(near):
    for target in near.values():
        pl.semaphore_signal(pltpu.get_barrier_semaphore(), inc=1, device_id=target, device_id_type=MESH)


def await_greetings(near):
    pl.semaphore_wait(pltpu.get_barrier_semaphore(), len(near))


class Copies:
    def __init__(self, near, send_sem, recv_sem):
        self.near, self.send_sem, self.recv_sem = near, send_sem, recv_sem
        self.started = []

    def start(self, source, target, to):
        k = len(self.started)
        copy = pltpu.make_async_remote_copy(
            src_ref=source,
            dst_ref=target,
            send_sem=self.send_sem.at[k],
            recv_sem=self.recv_sem.at[k],
            device_id=self.near[to],
            device_id_type=MESH,
        )
        copy.start()
        self.started.append(copy)
        return copy

    def finish(self):
        for copy in self.started:
            copy.wait_send()


GATHER_COPIES = 38
SCATTER_COPIES = 23


def gather_kernel(pos_hbm, type_hbm, params_hbm, row_ref, feat, mom, cen, vel, wid, table, col_ref, params_ref, pos_in, type_in, load_sem, send_sem, recv_sem):
    load_pos = pltpu.make_async_copy(pos_hbm, pos_in, load_sem.at[0])
    load_type = pltpu.make_async_copy(type_hbm, type_in, load_sem.at[1])
    load_params = pltpu.make_async_copy(params_hbm, params_ref, load_sem.at[2])
    load_pos.start()
    load_type.start()
    load_params.start()
    y, zl, zh, x, core = place()
    near = neighbours(y, zl, zh, x, core)
    greet(near)
    at = lambda xx, zz: core * 16 + zz * 4 + xx
    col_at = lambda yy, ll: yy * 2 + ll
    mine, col_mine, col_pal = at(x, zh), col_at(y, zl), col_at(y, 1 - zl)
    load_pos.wait()
    load_type.wait()
    for ref, slot in ((row_ref, mine), (col_ref, col_mine)):
        ref[slot, 0:3, :] = pos_in[...]
        for k in range(16):
            ref[slot, 3:4, k * TILE : (k + 1) * TILE] = type_in[k : k + 1, :].astype(F32)
    await_greetings(near)
    net = Copies(near, send_sem, recv_sem)

    def send(ref, slot, to):
        return net.start(ref.at[slot], ref.at[slot], to)

    along_z = {name: send(row_ref, mine, "z_" + name) for name in STEPS}
    along_x, along_y, twins = {}, {}, []
    pal = send(col_ref, col_mine, "pal")

    def pass_on(zz, key):
        along_x[key] = {name: send(row_ref, at(x, zz), "x_" + name) for name in STEPS}
        twins.append(send(row_ref, at(x, zz), "twin"))

    def pass_col(slot, key):
        along_y[key] = {name: send(col_ref, slot, "y_" + name) for name in STEPS}

    def hand_over(zz, key):
        for name in ("up", "down", "far"):
            along_x[key][name].wait_recv()
            twins.append(send(row_ref, at(ring(x, -STEPS[name]), zz), "twin"))

    pass_on(zh, "own")
    pass_col(col_mine, 0)
    load_params.wait()
    table[...] = jnp.zeros_like(table)
    for k in range(4):
        table[k : k + 1, 0:NTYPES] = jnp.sqrt(params_ref[0:1, :])
        table[k + 4 : k + 5, 0:NTYPES] = params_ref[1:2, :] * WIDTH_SCALE
    prepare = column_preparer(table, col_ref, feat, mom, cen, vel, wid)
    prepare(col_mine)
    pal.wait_recv()
    pass_col(col_pal, 1)
    for name in ("up", "down"):
        along_z[name].wait_recv()
        pass_on(ring(zh, -STEPS[name]), name)
    prepare(col_pal)
    hand_over(zh, "own")
    along_z["far"].wait_recv()
    pass_on(ring(zh, 2), "far")
    for name in ("up", "down"):
        along_y[0][name].wait_recv()
        prepare(col_at(ring(y, -STEPS[name]), zl))
    hand_over(ring(zh, -1), "up")
    hand_over(ring(zh, 1), "down")
    for name in ("up", "down"):
        along_y[1][name].wait_recv()
        prepare(col_at(ring(y, -STEPS[name]), 1 - zl))
    hand_over(ring(zh, 2), "far")
    for key, ll in ((0, zl), (1, 1 - zl)):
        along_y[key]["far"].wait_recv()
        prepare(col_at(ring(y, 2), ll))
    for copy in twins:
        copy.wait_recv()
    net.finish()


def in_hbm(array):
    return pltpu.with_memory_space_constraint(array, pltpu.HBM)


def gather(positions, kinds, params):
    hbm = pl.BlockSpec(memory_space=pltpu.HBM)
    vmem = pl.BlockSpec(memory_space=pltpu.VMEM)
    out = lambda *shape: jax.ShapeDtypeStruct(shape, F32)
    row_data, *columns = pl.pallas_call(
        gather_kernel,
        out_shape=(
            out(32, 4, 2048),
            jax.ShapeDtypeStruct((COL_TILES, TILE, TILE), BF16),
            out(COL_TILES, 8, TILE),
            out(COL_TILES, 8, TILE),
            out(COL_TILES, 8, TILE),
            out(COL_TILES, TILE, TILE),
            out(8, TILE),
        ),
        in_specs=[hbm] * 3,
        out_specs=(vmem,) * 7,
        scratch_shapes=[
            pltpu.VMEM((8, 4, 2048), F32),
            pltpu.VMEM((2, NTYPES), F32),
            pltpu.VMEM((3, 2048), F32),
            pltpu.VMEM((16, TILE), jnp.int32),
            pltpu.SemaphoreType.DMA((3,)),
            pltpu.SemaphoreType.DMA((GATHER_COPIES,)),
            pltpu.SemaphoreType.DMA((GATHER_COPIES,)),
        ],
        compiler_params=pltpu.CompilerParams(
            collective_id=0, has_side_effects=True, vmem_limit_bytes=22 * 1024 * 1024
        ),
        name="gather_atoms",
    )(*map(in_hbm, (positions, kinds, params)))
    return row_data, columns


def scatter_kernel(row_ref, col_ref, out_ref, from_twin, row_sum, x_in, z_out, z_in, y_in, col_sum, pal_in, send_sem, recv_sem):
    y, zl, zh, x, core = place()
    near = neighbours(y, zl, zh, x, core)
    greet(near)
    await_greetings(near)
    net = Copies(near, send_sem, recv_sem)
    offsets = (2, 1, -1, 0)
    order = ("far", "up", "down")

    twins = []
    for d in offsets:
        rows = ring(zh, d) * 4
        twins.append(net.start(row_ref.at[pl.ds((1 - core) * 16 + rows, 4)], from_twin.at[pl.ds(rows, 4)], "twin"))
    along_y = [net.start(col_ref.at[pl.ds(ring(y, STEPS[n]) * 2, 2)], y_in.at[k], "y_" + n) for k, n in enumerate(order)]

    along_x = []
    for i, d in enumerate(offsets):
        rows = ring(zh, d) * 4
        twins[i].wait_recv()
        row_sum[pl.ds(rows, 4)] = row_ref[pl.ds(core * 16 + rows, 4)] + from_twin[pl.ds(rows, 4)]
        along_x.append(
            [net.start(row_sum.at[rows + ring(x, STEPS[n])], x_in.at[i, k], "x_" + n) for k, n in enumerate(order)]
        )

    for copy in along_y:
        copy.wait_recv()
    here = y * 2
    col_sum[0] = col_ref[here + 1 - zl] + y_in[0, 1 - zl] + y_in[1, 1 - zl] + y_in[2, 1 - zl]
    pal = net.start(col_sum.at[0], pal_in, "pal")
    col_sum[1] = col_ref[here + zl] + y_in[0, zl] + y_in[1, zl] + y_in[2, zl]

    along_z = []
    for i, d in enumerate(offsets):
        for copy in along_x[i]:
            copy.wait_recv()
        total = row_sum[ring(zh, d) * 4 + x] + x_in[i, 0] + x_in[i, 1] + x_in[i, 2]
        if d:
            z_out[i] = total
            along_z.append(net.start(z_out.at[i], z_in.at[i], "z_" + order[i]))
        else:
            col_sum[1] = col_sum[1] + total
    pal.wait_recv()
    col_sum[1] = col_sum[1] + pal_in[...]
    for copy in along_z:
        copy.wait_recv()
    col_sum[1] = col_sum[1] + (z_in[0] + z_in[1] + z_in[2])
    for c in range(3):
        for k in range(16):
            out_ref[c : c + 1, k * TILE : (k + 1) * TILE] = col_sum[1, c * 16 + k : c * 16 + k + 1, :]
    net.finish()


def scatter(row_part, col_part):
    vmem = pl.BlockSpec(memory_space=pltpu.VMEM)
    block = lambda *n: pltpu.VMEM((*n, 48, TILE), F32)
    return pl.pallas_call(
        scatter_kernel,
        out_shape=jax.ShapeDtypeStruct((3, 2048), F32),
        in_specs=[vmem, vmem],
        out_specs=vmem,
        scratch_shapes=[
            block(16),
            block(16),
            block(4, 3),
            block(3),
            block(3),
            block(3, 2),
            block(2),
            block(),
            pltpu.SemaphoreType.DMA((SCATTER_COPIES,)),
            pltpu.SemaphoreType.DMA((SCATTER_COPIES,)),
        ],
        compiler_params=pltpu.CompilerParams(
            collective_id=1, has_side_effects=True, vmem_limit_bytes=10 * 1024 * 1024
        ),
        name="scatter_forces",
    )(row_part, col_part)


def shards(positions, type_ids, type_params, pair_tiles, pair_counts):
    row_data, columns = gather(positions, type_ids.reshape(16, TILE), type_params)
    tiles = pair_tiles[0, 0].T
    row_part, col_part = forces_of(pair_counts, in_hbm(tiles), row_data, *columns)
    return scatter(row_part, col_part)


def solution(mesh):
    placed = (
        P(None, ("row", "col")),
        P(("row", "col")),
        P(),
        P("row", "col", None, None),
        P("row", "col"),
    )
    return jax.shard_map(
        shards, mesh=mesh, in_specs=placed, out_specs=P(None, ("row", "col")), check_vma=False
    )
```

```python
import math

import jax
import jax.numpy as jnp
from jax import lax
from jax.experimental import pallas as pl
from jax.experimental.pallas import tpu as pltpu
from jax.sharding import PartitionSpec as P

TILE = 128
NTYPES = 16
CUTOFF_SQ = 6.25
LOG2E = math.log2(math.e)
KAPPA = 2.0 / (CUTOFF_SQ * LOG2E)
WIDTH_SCALE = 0.5 / math.sqrt(CUTOFF_SQ * LOG2E)
GROUP = 8
TURNS = 5
CHUNK = 32
UNROLL = GROUP * TURNS
G2 = 2 * GROUP
U2 = GROUP
FIRST = 128
ROW_TILES = 512
COL_TILES = 128
F32 = jnp.float32
BF16 = jnp.bfloat16
MESH = pl.DeviceIdType.MESH


def pieces(value):
    high = value.astype(BF16).astype(F32)
    rest = value - high
    middle = rest.astype(BF16).astype(F32)
    return high, middle, rest, rest - middle


def distance_stack(value, order):
    high, middle, _, low = pieces(value)
    part = {"h": high, "m": middle, "l": low}
    return [jnp.concatenate([part[order[k]], part[order[k + 1]]], axis=0).astype(BF16) for k in (0, 2, 4)]


def moment_stack(value, upper):
    high = value.astype(BF16).astype(F32)
    return jnp.where(upper, high, value - high)


def look_up(table, kind):
    both = jnp.take_along_axis(table, kind.astype(jnp.int32), axis=1)
    return jnp.broadcast_to(both[0:1], (8, TILE)), jnp.broadcast_to(both[4:5], (8, TILE))


def wide(ref, dev, comp, lane):
    return jnp.broadcast_to(ref[dev, comp : comp + 1, pl.ds(lane, TILE)], (8, TILE))


def spread(quad, x, y, z, last):
    return jnp.where(quad == 0, x, jnp.where(quad == 1, y, jnp.where(quad == 2, z, last)))


def column_preparer(table, col_ref, feat, mom, cen, vel, wid):
    sub = lax.broadcasted_iota(jnp.int32, (8, TILE), 0)
    quad = sub & 3
    zero8 = jnp.zeros((8, TILE), F32)
    types = table[...]
    zeros = jnp.zeros((64, TILE), BF16)
    row = lax.broadcasted_iota(jnp.int32, (TILE, TILE), 0)
    pick = jnp.where((row >= 48) & (row < 51), 1.0, 0.0).astype(BF16)

    def prepare(dev, k):
        b = dev * 16 + k
        x, y, z, kind = (wide(col_ref, dev, c, k * TILE) for c in range(4))
        here = spread(quad, x, y, z, 0.0)
        centre = jnp.sum(here, axis=1, keepdims=True) * (1.0 / TILE)
        cen[b] = jnp.broadcast_to(centre, (8, TILE))
        v = here - centre
        norm = jnp.sum(jnp.where(sub < 3, v * v, 0.0), axis=0, keepdims=True)
        depth, width = look_up(types, kind)
        z8 = jnp.where(sub < 3, v * (2.0 / CUTOFF_SQ), jnp.where(sub == 3, 1.0, jnp.where(sub == 4, norm * (-1.0 / CUTOFF_SQ), 0.0)))
        high, middle, _, low = pieces(width)
        widths = jnp.where(sub == 0, high, jnp.where(sub == 1, middle, jnp.where(sub == 2, low, 0.0)))
        widths = jnp.concatenate([widths, zero8], axis=0).astype(BF16)
        turned = jnp.concatenate(distance_stack(z8, "hmlhmh") + [widths, zeros], axis=0).T
        feat[b] = turned
        wid[b] = jnp.dot(turned, pick, preferred_element_type=F32)
        mom[b] = moment_stack(jnp.where(quad == 3, 1.0, v) * depth, sub < 4)
        vel[b] = jnp.where(sub == 3, depth * KAPPA, v)

    def shard(dev):
        for k in range(16):
            prepare(dev, k)

    return shard


def force_kernel(count_ref, tiles_hbm, row_ref, feat, mom, cen, vel, wid, table, row_out, col_out, acc_row, acc_col, slope, mine, offset, scale, span, reach, tiles_ref, load_sem):
    load_tiles = pltpu.make_async_copy(tiles_hbm, tiles_ref.at[:, pl.ds(FIRST, 384)], load_sem)
    load_tiles.start()
    sub = lax.broadcasted_iota(jnp.int32, (8, TILE), 0)
    quad = sub & 3
    upper = sub < 4
    unit = jnp.where(sub == 4, 1.0, 0.0)
    types = table[...]
    zeros80 = jnp.zeros((80, TILE), BF16)
    zeros128 = jnp.zeros((TILE, TILE), BF16)
    acc_row[...] = jnp.zeros_like(acc_row)
    acc_col[...] = jnp.zeros_like(acc_col)
    load_tiles.wait()
    count = count_ref[0, 0]
    for k in range(-2 * GROUP, 6 * GROUP):
        at = FIRST + k + (0 if k < 0 else count)
        tiles_ref[0, at] = ROW_TILES
        tiles_ref[1, at] = COL_TILES

    def fold(out):
        return out + pltpu.roll(out, 4, 0)

    def nearness(slot, k):
        a, b = tiles_ref[0, slot] & (ROW_TILES - 1), tiles_ref[1, slot] & (COL_TILES - 1)
        dev = (a & 16) + (a >> 5)
        lane = pl.multiple_of((a & 15) * TILE, TILE)
        x, y, z = (wide(row_ref, dev, c, lane) - jnp.broadcast_to(cen[b, c : c + 1, :], (8, TILE)) for c in range(3))
        kind = wide(row_ref, dev, 3, lane)
        depth, width = look_up(types, kind)
        q = 1.0 - (x * x + y * y + z * z) * (1.0 / CUTOFF_SQ)
        xz = spread(quad, x, y, z, 1.0)
        z8 = jnp.where(sub < 3, xz, jnp.where(sub == 3, q, unit))
        mine[k][...] = moment_stack(xz * depth, upper)
        offset[k][...] = xz
        scale[k][...] = depth * KAPPA
        span[k][...] = width
        return b, jnp.concatenate(distance_stack(z8, "hhhmml") + [zeros80], axis=0)

    def measure(slot, k):
        sides = [nearness(slot + n, k + n) for n in range(2)]
        feats = jnp.concatenate([feat[b] for b, _ in sides], axis=1)
        first, second = (near for _, near in sides)
        weights = jnp.concatenate(
            [jnp.concatenate([first, zeros128], axis=1), jnp.concatenate([zeros128, second], axis=1)], axis=0
        )
        reach[k // 2 % U2][...] = jnp.dot(feats, weights, preferred_element_type=F32)

    def spread_out(slot, k):
        b = tiles_ref[1, slot] & (COL_TILES - 1)
        half = (k % 2) * TILE
        for low in range(0, TILE, CHUNK):
            c = jnp.maximum(reach[k // 2 % U2][low : low + CHUNK, half : half + TILE], 0.0)
            spans = wid[b, low : low + CHUNK, :].reshape(CHUNK // 8, 8, TILE) + span[k][...][None]
            inverse = pl.reciprocal(spans.reshape(CHUNK, TILE), approx=True)
            decay = inverse * inverse
            u = c * decay
            g = (c * (u + 2.0 * LOG2E)) * jnp.exp2(u - decay)
            g_high = g.astype(BF16)
            slope[k % G2][low : low + CHUNK, :] = g_high
            slope[k % G2][TILE + low : TILE + low + CHUNK, :] = (g - g_high.astype(F32)).astype(BF16)

    def gather_in(slot, k):
        a, b = tiles_ref[0, slot], tiles_ref[1, slot]
        a_to, b_to = pl.multiple_of(a * 8, 8), pl.multiple_of(b * 8, 8)
        sides = jnp.concatenate([mom[b & (COL_TILES - 1)], mine[k][...]], axis=0).astype(BF16)
        g = slope[k % G2][...]
        across = jnp.concatenate([g[:TILE].T, g[TILE:].T], axis=0)
        out = jnp.dot(
            jnp.concatenate([sides, sides], axis=1),
            jnp.concatenate([g, across], axis=1),
            preferred_element_type=F32,
        )
        to_i = fold(out[0:8, :TILE])
        to_j = fold(out[8:16, TILE:])
        weight = jnp.broadcast_to(to_i[3:4], (8, TILE))
        on_i = (offset[k][...] * weight - to_i) * scale[k][...]
        return a_to, b_to, on_i, to_j

    def collect(slot, k):
        a_to, b_to, on_i, to_j = gather_in(slot, k)
        acc_row[pl.ds(a_to, 8), :] += on_i
        acc_col[pl.ds(b_to, 8), :] += to_j

    @pl.loop(0, pl.cdiv(pl.cdiv(count, GROUP) + 2, TURNS))
    def _(turn):
        base = FIRST + turn * (TURNS * GROUP)
        for h in range(TURNS):
            for n in range(GROUP):
                collect(base + (h - 2) * GROUP + n, (h - 2) % TURNS * GROUP + n)
                spread_out(base + (h - 1) * GROUP + n, (h - 1) % TURNS * GROUP + n)
                if n % 2:
                    measure(base + h * GROUP + n - 1, h * GROUP + n - 1)

    @pl.loop(0, COL_TILES, step=4)
    def _(b0):
        for k in range(4):
            b = b0 + k
            at = pl.multiple_of(b * 8, 8)
            got = acc_col[pl.ds(at, 8), :]
            v = vel[b]
            weight = jnp.broadcast_to(got[3:4], (8, TILE))
            depth = jnp.broadcast_to(v[3:4], (8, TILE))
            acc_col[pl.ds(at, 8), :] = (v * weight - got) * depth

    for q in range(32):
        slot = (q & 1) * 16 + (q >> 1)
        for c in range(3):
            row_out[slot, c * 16 : c * 16 + 16, :] = acc_row[pl.ds(q * 128 + c, 16, stride=8), :]
    for p in range(8):
        for c in range(3):
            col_out[p, c * 16 : c * 16 + 16, :] = acc_col[pl.ds(p * 128 + c, 16, stride=8), :]


def forces_of(count, tiles, row_data, *columns):
    hbm = pl.BlockSpec(memory_space=pltpu.HBM)
    vmem = pl.BlockSpec(memory_space=pltpu.VMEM)
    return pl.pallas_call(
        force_kernel,
        out_shape=(jax.ShapeDtypeStruct((32, 48, TILE), F32), jax.ShapeDtypeStruct((8, 48, TILE), F32)),
        in_specs=[pl.BlockSpec(memory_space=pltpu.SMEM), hbm] + [vmem] * 7,
        out_specs=(vmem, vmem),
        scratch_shapes=[
            pltpu.VMEM(((ROW_TILES + 1) * 8, TILE), F32),
            pltpu.VMEM(((COL_TILES + 1) * 8, TILE), F32),
            [pltpu.VMEM((2 * TILE, TILE), BF16)] * G2,
            [pltpu.VMEM((8, TILE), F32)] * UNROLL,
            [pltpu.VMEM((8, TILE), F32)] * UNROLL,
            [pltpu.VMEM((8, TILE), F32)] * UNROLL,
            [pltpu.VMEM((8, TILE), F32)] * UNROLL,
            [pltpu.VMEM((TILE, 2 * TILE), F32)] * U2,
            pltpu.SMEM((2, FIRST + 384 + 128), jnp.int32),
            pltpu.SemaphoreType.DMA,
        ],
        compiler_params=pltpu.CompilerParams(vmem_limit_bytes=26 * 1024 * 1024),
        name="pair_forces",
    )(count, tiles, row_data, *columns)


def ring(v, d):
    return (v + d + 4) % 4


def place():
    p, q = lax.axis_index("row"), lax.axis_index("col")
    return p // 2, p % 2, q // 8, (q // 2) % 4, q % 2


def device(y, zl, zh, x, core):
    return (y * 2 + zl, zh * 8 + x * 2 + core)


STEPS = {"far": 2, "up": 1, "down": -1}


def neighbours(y, zl, zh, x, core):
    near = {"twin": device(y, zl, zh, x, 1 - core), "pal": device(y, 1 - zl, zh, x, core)}
    for name, d in STEPS.items():
        near["z_" + name] = device(y, zl, ring(zh, d), x, core)
        near["x_" + name] = device(y, zl, zh, ring(x, d), core)
        near["y_" + name] = device(ring(y, d), zl, zh, x, core)
    return near


def greet(near):
    for target in near.values():
        pl.semaphore_signal(pltpu.get_barrier_semaphore(), inc=1, device_id=target, device_id_type=MESH)


def await_greetings(near):
    pl.semaphore_wait(pltpu.get_barrier_semaphore(), len(near))


class Copies:
    def __init__(self, near, send_sem, recv_sem):
        self.near, self.send_sem, self.recv_sem = near, send_sem, recv_sem
        self.started = []

    def start(self, source, target, to):
        k = len(self.started)
        copy = pltpu.make_async_remote_copy(
            src_ref=source,
            dst_ref=target,
            send_sem=self.send_sem.at[k],
            recv_sem=self.recv_sem.at[k],
            device_id=self.near[to],
            device_id_type=MESH,
        )
        copy.start()
        self.started.append(copy)
        return copy

    def finish(self):
        for copy in self.started:
            copy.wait_send()


GATHER_COPIES = 38
SCATTER_COPIES = 23


def gather_kernel(pos_hbm, type_hbm, params_hbm, row_ref, feat, mom, cen, vel, wid, table, col_ref, params_ref, pos_in, type_in, load_sem, send_sem, recv_sem):
    load_pos = pltpu.make_async_copy(pos_hbm, pos_in, load_sem.at[0])
    load_type = pltpu.make_async_copy(type_hbm, type_in, load_sem.at[1])
    load_params = pltpu.make_async_copy(params_hbm, params_ref, load_sem.at[2])
    load_pos.start()
    load_type.start()
    load_params.start()
    y, zl, zh, x, core = place()
    near = neighbours(y, zl, zh, x, core)
    greet(near)
    at = lambda xx, zz: core * 16 + zz * 4 + xx
    col_at = lambda yy, ll: yy * 2 + ll
    mine, col_mine, col_pal = at(x, zh), col_at(y, zl), col_at(y, 1 - zl)
    load_pos.wait()
    load_type.wait()
    for ref, slot in ((row_ref, mine), (col_ref, col_mine)):
        ref[slot, 0:3, :] = pos_in[...]
        for k in range(16):
            ref[slot, 3:4, k * TILE : (k + 1) * TILE] = type_in[k : k + 1, :].astype(F32)
    await_greetings(near)
    net = Copies(near, send_sem, recv_sem)

    def send(ref, slot, to):
        return net.start(ref.at[slot], ref.at[slot], to)

    along_z = {name: send(row_ref, mine, "z_" + name) for name in STEPS}
    along_x, along_y, twins = {}, {}, []
    pal = send(col_ref, col_mine, "pal")

    def pass_on(zz, key):
        names = ("up", "down") if key in ("up", "down") else STEPS
        along_x[key] = {name: send(row_ref, at(x, zz), "x_" + name) for name in names}
        twins.append(send(row_ref, at(x, zz), "twin"))

    def pass_col(slot, key):
        along_y[key] = {name: send(col_ref, slot, "y_" + name) for name in STEPS}

    def hand_over(zz, key, names):
        for name in names:
            along_x[key][name].wait_recv()
            twins.append(send(row_ref, at(ring(x, -STEPS[name]), zz), "twin"))

    pass_on(zh, "own")
    pass_col(col_mine, 0)
    load_params.wait()
    table[...] = jnp.zeros_like(table)
    for k in range(4):
        table[k : k + 1, 0:NTYPES] = jnp.sqrt(params_ref[0:1, :])
        table[k + 4 : k + 5, 0:NTYPES] = params_ref[1:2, :] * WIDTH_SCALE
    prepare = column_preparer(table, col_ref, feat, mom, cen, vel, wid)
    prepare(col_mine)
    pal.wait_recv()
    pass_col(col_pal, 1)
    along_x["own"]["far"].wait_recv()
    across = {name: send(row_ref, at(ring(x, 2), zh), "z_" + name) for name in ("up", "down")}
    twins.append(send(row_ref, at(ring(x, 2), zh), "twin"))
    for name in ("up", "down"):
        along_z[name].wait_recv()
        pass_on(ring(zh, -STEPS[name]), name)
    hand_over(zh, "own", ("up", "down"))
    along_z["far"].wait_recv()
    pass_on(ring(zh, 2), "far")
    prepare(col_pal)
    for name in ("up", "down"):
        along_y[0][name].wait_recv()
        prepare(col_at(ring(y, -STEPS[name]), zl))
    for name in ("up", "down"):
        zz = ring(zh, -STEPS[name])
        hand_over(zz, name, ("up", "down"))
        across[name].wait_recv()
        twins.append(send(row_ref, at(ring(x, 2), zz), "twin"))
    for name in ("up", "down"):
        along_y[1][name].wait_recv()
        prepare(col_at(ring(y, -STEPS[name]), 1 - zl))
    hand_over(ring(zh, 2), "far", ("up", "down", "far"))
    for key, ll in ((0, zl), (1, 1 - zl)):
        along_y[key]["far"].wait_recv()
        prepare(col_at(ring(y, 2), ll))
    for copy in twins:
        copy.wait_recv()
    net.finish()


def in_hbm(array):
    return pltpu.with_memory_space_constraint(array, pltpu.HBM)


def gather(positions, kinds, params):
    hbm = pl.BlockSpec(memory_space=pltpu.HBM)
    vmem = pl.BlockSpec(memory_space=pltpu.VMEM)
    out = lambda *shape: jax.ShapeDtypeStruct(shape, F32)
    row_data, *columns = pl.pallas_call(
        gather_kernel,
        out_shape=(
            out(32, 4, 2048),
            jax.ShapeDtypeStruct((COL_TILES, TILE, TILE), BF16),
            out(COL_TILES, 8, TILE),
            out(COL_TILES, 8, TILE),
            out(COL_TILES, 8, TILE),
            out(COL_TILES, TILE, TILE),
            out(8, TILE),
        ),
        in_specs=[hbm] * 3,
        out_specs=(vmem,) * 7,
        scratch_shapes=[
            pltpu.VMEM((8, 4, 2048), F32),
            pltpu.VMEM((2, NTYPES), F32),
            pltpu.VMEM((3, 2048), F32),
            pltpu.VMEM((16, TILE), jnp.int32),
            pltpu.SemaphoreType.DMA((3,)),
            pltpu.SemaphoreType.DMA((GATHER_COPIES,)),
            pltpu.SemaphoreType.DMA((GATHER_COPIES,)),
        ],
        compiler_params=pltpu.CompilerParams(
            collective_id=0, has_side_effects=True, vmem_limit_bytes=22 * 1024 * 1024
        ),
        name="gather_atoms",
    )(*map(in_hbm, (positions, kinds, params)))
    return row_data, columns


def scatter_kernel(row_ref, col_ref, out_ref, from_twin, row_sum, x_in, z_out, z_in, y_in, col_sum, pal_in, send_sem, recv_sem):
    y, zl, zh, x, core = place()
    near = neighbours(y, zl, zh, x, core)
    greet(near)
    await_greetings(near)
    net = Copies(near, send_sem, recv_sem)
    offsets = (2, 1, -1, 0)
    order = ("far", "up", "down")

    twins = []
    for d in offsets:
        rows = ring(zh, d) * 4
        twins.append(net.start(row_ref.at[pl.ds((1 - core) * 16 + rows, 4)], from_twin.at[pl.ds(rows, 4)], "twin"))
    along_y = [net.start(col_ref.at[pl.ds(ring(y, STEPS[n]) * 2, 2)], y_in.at[k], "y_" + n) for k, n in enumerate(order)]

    along_x = []
    for i, d in enumerate(offsets):
        rows = ring(zh, d) * 4
        twins[i].wait_recv()
        row_sum[pl.ds(rows, 4)] = row_ref[pl.ds(core * 16 + rows, 4)] + from_twin[pl.ds(rows, 4)]
        along_x.append(
            [net.start(row_sum.at[rows + ring(x, STEPS[n])], x_in.at[i, k], "x_" + n) for k, n in enumerate(order)]
        )

    for copy in along_y:
        copy.wait_recv()
    here = y * 2
    col_sum[0] = col_ref[here + 1 - zl] + y_in[0, 1 - zl] + y_in[1, 1 - zl] + y_in[2, 1 - zl]
    pal = net.start(col_sum.at[0], pal_in, "pal")
    col_sum[1] = col_ref[here + zl] + y_in[0, zl] + y_in[1, zl] + y_in[2, zl]

    along_z = []
    for i, d in enumerate(offsets):
        for copy in along_x[i]:
            copy.wait_recv()
        total = row_sum[ring(zh, d) * 4 + x] + x_in[i, 0] + x_in[i, 1] + x_in[i, 2]
        if d:
            z_out[i] = total
            along_z.append(net.start(z_out.at[i], z_in.at[i], "z_" + order[i]))
        else:
            col_sum[1] = col_sum[1] + total
    pal.wait_recv()
    col_sum[1] = col_sum[1] + pal_in[...]
    for copy in along_z:
        copy.wait_recv()
    col_sum[1] = col_sum[1] + (z_in[0] + z_in[1] + z_in[2])
    for c in range(3):
        for k in range(16):
            out_ref[c : c + 1, k * TILE : (k + 1) * TILE] = col_sum[1, c * 16 + k : c * 16 + k + 1, :]
    net.finish()


def scatter(row_part, col_part):
    vmem = pl.BlockSpec(memory_space=pltpu.VMEM)
    block = lambda *n: pltpu.VMEM((*n, 48, TILE), F32)
    return pl.pallas_call(
        scatter_kernel,
        out_shape=jax.ShapeDtypeStruct((3, 2048), F32),
        in_specs=[vmem, vmem],
        out_specs=vmem,
        scratch_shapes=[
            block(16),
            block(16),
            block(4, 3),
            block(3),
            block(3),
            block(3, 2),
            block(2),
            block(),
            pltpu.SemaphoreType.DMA((SCATTER_COPIES,)),
            pltpu.SemaphoreType.DMA((SCATTER_COPIES,)),
        ],
        compiler_params=pltpu.CompilerParams(
            collective_id=1, has_side_effects=True, vmem_limit_bytes=10 * 1024 * 1024
        ),
        name="scatter_forces",
    )(row_part, col_part)


def shards(positions, type_ids, type_params, pair_tiles, pair_counts):
    row_data, columns = gather(positions, type_ids.reshape(16, TILE), type_params)
    tiles = pair_tiles[0, 0].T
    row_part, col_part = forces_of(pair_counts, in_hbm(tiles), row_data, *columns)
    return scatter(row_part, col_part)


def solution(mesh):
    placed = (
        P(None, ("row", "col")),
        P(("row", "col")),
        P(),
        P("row", "col", None, None),
        P("row", "col"),
    )
    return jax.shard_map(
        shards, mesh=mesh, in_specs=placed, out_specs=P(None, ("row", "col")), check_vma=False
    )
```

```python
import math

import jax
import jax.numpy as jnp
from jax import lax
from jax.experimental import pallas as pl
from jax.experimental.pallas import tpu as pltpu
from jax.sharding import PartitionSpec as P

TILE = 128
NTYPES = 16
CUTOFF_SQ = 6.25
LOG2E = math.log2(math.e)
KAPPA = 2.0 / (CUTOFF_SQ * LOG2E)
WIDTH_SCALE = 0.5 / math.sqrt(CUTOFF_SQ * LOG2E)
GROUP = 8
TURNS = 5
CHUNK = 32
UNROLL = GROUP * TURNS
G2 = 2 * GROUP
U2 = GROUP
FIRST = 128
ROW_TILES = 512
COL_TILES = 128
F32 = jnp.float32
BF16 = jnp.bfloat16
MESH = pl.DeviceIdType.MESH


def pieces(value):
    high = value.astype(BF16).astype(F32)
    rest = value - high
    middle = rest.astype(BF16).astype(F32)
    return high, middle, rest, rest - middle


def distance_stack(value, order):
    high, middle, _, low = pieces(value)
    part = {"h": high, "m": middle, "l": low}
    return [jnp.concatenate([part[order[k]], part[order[k + 1]]], axis=0).astype(BF16) for k in (0, 2, 4)]


def moment_stack(value, upper):
    high = value.astype(BF16).astype(F32)
    return jnp.where(upper, high, value - high)


def look_up(table, kind):
    both = jnp.take_along_axis(table, kind.astype(jnp.int32), axis=1)
    return jnp.broadcast_to(both[0:1], (8, TILE)), jnp.broadcast_to(both[4:5], (8, TILE))


def wide(ref, dev, comp, lane):
    return jnp.broadcast_to(ref[dev, comp : comp + 1, pl.ds(lane, TILE)], (8, TILE))


def spread(quad, x, y, z, last):
    return jnp.where(quad == 0, x, jnp.where(quad == 1, y, jnp.where(quad == 2, z, last)))


def column_preparer(table, col_ref, feat, mom, cen, vel, wid):
    sub = lax.broadcasted_iota(jnp.int32, (8, TILE), 0)
    quad = sub & 3
    zero8 = jnp.zeros((8, TILE), F32)
    types = table[...]
    zeros = jnp.zeros((64, TILE), BF16)
    row = lax.broadcasted_iota(jnp.int32, (TILE, TILE), 0)
    pick = jnp.where((row >= 48) & (row < 51), 1.0, 0.0).astype(BF16)

    def prepare(dev, k):
        b = dev * 16 + k
        x, y, z, kind = (wide(col_ref, dev, c, k * TILE) for c in range(4))
        here = spread(quad, x, y, z, 0.0)
        centre = jnp.sum(here, axis=1, keepdims=True) * (1.0 / TILE)
        cen[b] = jnp.broadcast_to(centre, (8, TILE))
        v = here - centre
        norm = jnp.sum(jnp.where(sub < 3, v * v, 0.0), axis=0, keepdims=True)
        depth, width = look_up(types, kind)
        z8 = jnp.where(sub < 3, v * (2.0 / CUTOFF_SQ), jnp.where(sub == 3, 1.0, jnp.where(sub == 4, norm * (-1.0 / CUTOFF_SQ), 0.0)))
        high, middle, _, low = pieces(width)
        widths = jnp.where(sub == 0, high, jnp.where(sub == 1, middle, jnp.where(sub == 2, low, 0.0)))
        widths = jnp.concatenate([widths, zero8], axis=0).astype(BF16)
        turned = jnp.concatenate(distance_stack(z8, "hmlhmh") + [widths, zeros], axis=0).T
        feat[b] = turned
        wid[b] = jnp.dot(turned, pick, preferred_element_type=F32)
        mom[b] = moment_stack(jnp.where(quad == 3, 1.0, v) * depth, sub < 4)
        vel[b] = jnp.where(sub == 3, depth * KAPPA, v)

    def shard(dev):
        for k in range(16):
            prepare(dev, k)

    return shard


def force_kernel(count_ref, tiles_in, row_ref, feat, mom, cen, vel, wid, table, row_out, col_out, acc_row, acc_col, slope, mine, offset, scale, span, reach, tiles_ref, load_sem):
    load_tiles = pltpu.make_async_copy(tiles_in, tiles_ref.at[:, pl.ds(FIRST, 384)], load_sem)
    load_tiles.start()
    sub = lax.broadcasted_iota(jnp.int32, (8, TILE), 0)
    quad = sub & 3
    upper = sub < 4
    unit = jnp.where(sub == 4, 1.0, 0.0)
    types = table[...]
    zeros80 = jnp.zeros((80, TILE), BF16)
    zeros128 = jnp.zeros((TILE, TILE), BF16)
    acc_row[...] = jnp.zeros_like(acc_row)
    acc_col[...] = jnp.zeros_like(acc_col)
    load_tiles.wait()
    count = count_ref[0, 0]
    for k in range(-2 * GROUP, 6 * GROUP):
        at = FIRST + k + (0 if k < 0 else count)
        tiles_ref[0, at] = ROW_TILES
        tiles_ref[1, at] = COL_TILES

    def fold(out):
        return out + pltpu.roll(out, 4, 0)

    def nearness(slot, k):
        a, b = tiles_ref[0, slot] & (ROW_TILES - 1), tiles_ref[1, slot] & (COL_TILES - 1)
        dev = (a & 16) + (a >> 5)
        lane = pl.multiple_of((a & 15) * TILE, TILE)
        x, y, z = (wide(row_ref, dev, c, lane) - jnp.broadcast_to(cen[b, c : c + 1, :], (8, TILE)) for c in range(3))
        kind = wide(row_ref, dev, 3, lane)
        depth, width = look_up(types, kind)
        q = 1.0 - (x * x + y * y + z * z) * (1.0 / CUTOFF_SQ)
        xz = spread(quad, x, y, z, 1.0)
        z8 = jnp.where(sub < 3, xz, jnp.where(sub == 3, q, unit))
        mine[k][...] = moment_stack(xz * depth, upper)
        offset[k][...] = xz
        scale[k][...] = depth * KAPPA
        span[k][...] = width
        return b, jnp.concatenate(distance_stack(z8, "hhhmml") + [zeros80], axis=0)

    def measure(slot, k):
        sides = [nearness(slot + n, k + n) for n in range(2)]
        feats = jnp.concatenate([feat[b] for b, _ in sides], axis=1)
        first, second = (near for _, near in sides)
        weights = jnp.concatenate(
            [jnp.concatenate([first, zeros128], axis=1), jnp.concatenate([zeros128, second], axis=1)], axis=0
        )
        reach[k // 2 % U2][...] = jnp.dot(feats, weights, preferred_element_type=F32)

    def spread_out(slot, k):
        b = tiles_ref[1, slot] & (COL_TILES - 1)
        half = (k % 2) * TILE
        for low in range(0, TILE, CHUNK):
            c = jnp.maximum(reach[k // 2 % U2][low : low + CHUNK, half : half + TILE], 0.0)
            spans = wid[b, low : low + CHUNK, :].reshape(CHUNK // 8, 8, TILE) + span[k][...][None]
            inverse = pl.reciprocal(spans.reshape(CHUNK, TILE), approx=True)
            decay = inverse * inverse
            u = c * decay
            g = (c * (u + 2.0 * LOG2E)) * jnp.exp2(u - decay)
            g_high = g.astype(BF16)
            slope[k % G2][low : low + CHUNK, :] = g_high
            slope[k % G2][TILE + low : TILE + low + CHUNK, :] = (g - g_high.astype(F32)).astype(BF16)

    def gather_in(slot, k):
        a, b = tiles_ref[0, slot], tiles_ref[1, slot]
        a_to, b_to = pl.multiple_of(a * 8, 8), pl.multiple_of(b * 8, 8)
        sides = jnp.concatenate([mom[b & (COL_TILES - 1)], mine[k][...]], axis=0).astype(BF16)
        g = slope[k % G2][...]
        across = jnp.concatenate([g[:TILE].T, g[TILE:].T], axis=0)
        out = jnp.dot(
            jnp.concatenate([sides, sides], axis=1),
            jnp.concatenate([g, across], axis=1),
            preferred_element_type=F32,
        )
        to_i = fold(out[0:8, :TILE])
        to_j = fold(out[8:16, TILE:])
        weight = jnp.broadcast_to(to_i[3:4], (8, TILE))
        on_i = (offset[k][...] * weight - to_i) * scale[k][...]
        return a_to, b_to, on_i, to_j

    def collect(slot, k):
        a_to, b_to, on_i, to_j = gather_in(slot, k)
        acc_row[pl.ds(a_to, 8), :] += on_i
        acc_col[pl.ds(b_to, 8), :] += to_j

    @pl.loop(0, pl.cdiv(pl.cdiv(count, GROUP) + 2, TURNS))
    def _(turn):
        base = FIRST + turn * (TURNS * GROUP)
        for h in range(TURNS):
            for n in range(GROUP):
                collect(base + (h - 2) * GROUP + n, (h - 2) % TURNS * GROUP + n)
                spread_out(base + (h - 1) * GROUP + n, (h - 1) % TURNS * GROUP + n)
                if n % 2:
                    measure(base + h * GROUP + n - 1, h * GROUP + n - 1)

    @pl.loop(0, COL_TILES, step=16)
    def _(b0):
        for k in range(16):
            b = b0 + k
            at = pl.multiple_of(b * 8, 8)
            got = acc_col[pl.ds(at, 8), :]
            v = vel[b]
            weight = jnp.broadcast_to(got[3:4], (8, TILE))
            depth = jnp.broadcast_to(v[3:4], (8, TILE))
            acc_col[pl.ds(at, 8), :] = (v * weight - got) * depth

    for q in range(32):
        slot = (q & 1) * 16 + (q >> 1)
        for c in range(3):
            row_out[slot, c * 16 : c * 16 + 16, :] = acc_row[pl.ds(q * 128 + c, 16, stride=8), :]
    for p in range(8):
        for c in range(3):
            col_out[p, c * 16 : c * 16 + 16, :] = acc_col[pl.ds(p * 128 + c, 16, stride=8), :]


def forces_of(count, tiles, row_data, *columns):
    vmem = pl.BlockSpec(memory_space=pltpu.VMEM)
    return pl.pallas_call(
        force_kernel,
        out_shape=(jax.ShapeDtypeStruct((32, 48, TILE), F32), jax.ShapeDtypeStruct((8, 48, TILE), F32)),
        in_specs=[pl.BlockSpec(memory_space=pltpu.SMEM)] + [vmem] * 8,
        out_specs=(vmem, vmem),
        scratch_shapes=[
            pltpu.VMEM(((ROW_TILES + 1) * 8, TILE), F32),
            pltpu.VMEM(((COL_TILES + 1) * 8, TILE), F32),
            [pltpu.VMEM((2 * TILE, TILE), BF16)] * G2,
            [pltpu.VMEM((8, TILE), F32)] * UNROLL,
            [pltpu.VMEM((8, TILE), F32)] * UNROLL,
            [pltpu.VMEM((8, TILE), F32)] * UNROLL,
            [pltpu.VMEM((8, TILE), F32)] * UNROLL,
            [pltpu.VMEM((TILE, 2 * TILE), F32)] * U2,
            pltpu.SMEM((2, FIRST + 384 + 128), jnp.int32),
            pltpu.SemaphoreType.DMA,
        ],
        compiler_params=pltpu.CompilerParams(vmem_limit_bytes=26 * 1024 * 1024),
        name="pair_forces",
    )(count, tiles, row_data, *columns)


def ring(v, d):
    return (v + d + 4) % 4


def place():
    p, q = lax.axis_index("row"), lax.axis_index("col")
    return p // 2, p % 2, q // 8, (q // 2) % 4, q % 2


def device(y, zl, zh, x, core):
    return (y * 2 + zl, zh * 8 + x * 2 + core)


STEPS = {"far": 2, "up": 1, "down": -1}


def neighbours(y, zl, zh, x, core, cross=False):
    near = {"twin": device(y, zl, zh, x, 1 - core), "pal": device(y, 1 - zl, zh, x, core)}
    for name, d in STEPS.items():
        near["z_" + name] = device(y, zl, ring(zh, d), x, core)
        near["x_" + name] = device(y, zl, zh, ring(x, d), core)
        near["y_" + name] = device(ring(y, d), zl, zh, x, core)
        if cross:
            near["c_" + name] = device(y, zl, zh, ring(x, d), 1 - core)
    return near


def greet(near):
    for target in near.values():
        pl.semaphore_signal(pltpu.get_barrier_semaphore(), inc=1, device_id=target, device_id_type=MESH)


def await_greetings(near):
    pl.semaphore_wait(pltpu.get_barrier_semaphore(), len(near))


class Copies:
    def __init__(self, near, send_sem, recv_sem):
        self.near, self.send_sem, self.recv_sem = near, send_sem, recv_sem
        self.started = []

    def start(self, source, target, to):
        k = len(self.started)
        copy = pltpu.make_async_remote_copy(
            src_ref=source,
            dst_ref=target,
            send_sem=self.send_sem.at[k],
            recv_sem=self.recv_sem.at[k],
            device_id=self.near[to],
            device_id_type=MESH,
        )
        copy.start()
        self.started.append(copy)
        return copy

    def finish(self):
        for copy in self.started:
            copy.wait_send()


GATHER_COPIES = 38
SCATTER_COPIES = 26


def gather_kernel(pos_hbm, type_hbm, params_hbm, tiles_hbm, tiles_ref, row_ref, feat, mom, cen, vel, wid, table, col_ref, params_ref, pos_in, type_in, load_sem, send_sem, recv_sem):
    load_pos = pltpu.make_async_copy(pos_hbm, pos_in, load_sem.at[0])
    load_type = pltpu.make_async_copy(type_hbm, type_in, load_sem.at[1])
    load_params = pltpu.make_async_copy(params_hbm, params_ref, load_sem.at[2])
    load_pos.start()
    load_type.start()
    load_params.start()
    load_tiles = pltpu.make_async_copy(tiles_hbm, tiles_ref, load_sem.at[3])
    load_tiles.start()
    y, zl, zh, x, core = place()
    near = neighbours(y, zl, zh, x, core)
    greet(near)
    at = lambda xx, zz: core * 16 + zz * 4 + xx
    col_at = lambda yy, ll: yy * 2 + ll
    mine, col_mine, col_pal = at(x, zh), col_at(y, zl), col_at(y, 1 - zl)
    load_pos.wait()
    load_type.wait()
    for ref, slot in ((row_ref, mine), (col_ref, col_mine)):
        ref[slot, 0:3, :] = pos_in[...]
        for k in range(16):
            ref[slot, 3:4, k * TILE : (k + 1) * TILE] = type_in[k : k + 1, :].astype(F32)
    await_greetings(near)
    net = Copies(near, send_sem, recv_sem)

    def send(ref, slot, to):
        return net.start(ref.at[slot], ref.at[slot], to)

    along_z = {name: send(row_ref, mine, "z_" + name) for name in STEPS}
    along_x, along_y, twins = {}, {}, []
    pal = send(col_ref, col_mine, "pal")

    def pass_on(zz, key):
        names = ("up", "down") if key in ("up", "down") else STEPS
        along_x[key] = {name: send(row_ref, at(x, zz), "x_" + name) for name in names}
        twins.append(send(row_ref, at(x, zz), "twin"))

    def pass_col(slot, key):
        along_y[key] = {name: send(col_ref, slot, "y_" + name) for name in STEPS}

    def hand_over(zz, key, names):
        for name in names:
            along_x[key][name].wait_recv()
            twins.append(send(row_ref, at(ring(x, -STEPS[name]), zz), "twin"))

    pass_on(zh, "own")
    pass_col(col_mine, 0)
    load_params.wait()
    table[...] = jnp.zeros_like(table)
    for k in range(4):
        table[k : k + 1, 0:NTYPES] = jnp.sqrt(params_ref[0:1, :])
        table[k + 4 : k + 5, 0:NTYPES] = params_ref[1:2, :] * WIDTH_SCALE
    prepare = column_preparer(table, col_ref, feat, mom, cen, vel, wid)
    prepare(col_mine)
    pal.wait_recv()
    pass_col(col_pal, 1)
    along_x["own"]["far"].wait_recv()
    across = {name: send(row_ref, at(ring(x, 2), zh), "z_" + name) for name in ("up", "down")}
    twins.append(send(row_ref, at(ring(x, 2), zh), "twin"))
    for name in ("up", "down"):
        along_z[name].wait_recv()
        pass_on(ring(zh, -STEPS[name]), name)
    hand_over(zh, "own", ("up", "down"))
    prepare(col_pal)
    along_y[0]["up"].wait_recv()
    prepare(col_at(ring(y, -1), zl))
    along_z["far"].wait_recv()
    pass_on(ring(zh, 2), "far")
    along_y[0]["down"].wait_recv()
    prepare(col_at(ring(y, 1), zl))
    along_y[1]["up"].wait_recv()
    prepare(col_at(ring(y, -1), 1 - zl))
    for name in ("up", "down"):
        zz = ring(zh, -STEPS[name])
        hand_over(zz, name, ("up", "down"))
        across[name].wait_recv()
        twins.append(send(row_ref, at(ring(x, 2), zz), "twin"))
    along_y[1]["down"].wait_recv()
    prepare(col_at(ring(y, 1), 1 - zl))
    hand_over(ring(zh, 2), "far", ("up", "down", "far"))
    for key, ll in ((0, zl), (1, 1 - zl)):
        along_y[key]["far"].wait_recv()
        prepare(col_at(ring(y, 2), ll))
    load_tiles.wait()
    for copy in twins:
        copy.wait_recv()
    net.finish()


def in_hbm(array):
    return pltpu.with_memory_space_constraint(array, pltpu.HBM)


def gather(positions, kinds, params, tiles):
    hbm = pl.BlockSpec(memory_space=pltpu.HBM)
    vmem = pl.BlockSpec(memory_space=pltpu.VMEM)
    out = lambda *shape: jax.ShapeDtypeStruct(shape, F32)
    tiles, row_data, *columns = pl.pallas_call(
        gather_kernel,
        out_shape=(
            jax.ShapeDtypeStruct((2, 384), jnp.int32),
            out(32, 4, 2048),
            jax.ShapeDtypeStruct((COL_TILES, TILE, TILE), BF16),
            out(COL_TILES, 8, TILE),
            out(COL_TILES, 8, TILE),
            out(COL_TILES, 8, TILE),
            out(COL_TILES, TILE, TILE),
            out(8, TILE),
        ),
        in_specs=[hbm] * 4,
        out_specs=(vmem,) * 8,
        scratch_shapes=[
            pltpu.VMEM((8, 4, 2048), F32),
            pltpu.VMEM((2, NTYPES), F32),
            pltpu.VMEM((3, 2048), F32),
            pltpu.VMEM((16, TILE), jnp.int32),
            pltpu.SemaphoreType.DMA((4,)),
            pltpu.SemaphoreType.DMA((GATHER_COPIES,)),
            pltpu.SemaphoreType.DMA((GATHER_COPIES,)),
        ],
        compiler_params=pltpu.CompilerParams(
            collective_id=0, has_side_effects=True, vmem_limit_bytes=22 * 1024 * 1024
        ),
        name="gather_atoms",
    )(*map(in_hbm, (positions, kinds, params, tiles)))
    return tiles, row_data, columns


def scatter_kernel(row_ref, col_ref, out_ref, from_twin, row_sum, x_in, z_out, z_in, y_in, col_sum, pal_in, cross_in, send_sem, recv_sem):
    y, zl, zh, x, core = place()
    near = neighbours(y, zl, zh, x, core, cross=True)
    greet(near)
    await_greetings(near)
    net = Copies(near, send_sem, recv_sem)
    offsets = (2, 1, -1, 0)
    order = ("far", "up", "down")

    far = ring(zh, 2) * 4
    along_x = [[]]
    for k, n in enumerate(order):
        there = far + ring(x, STEPS[n])
        along_x[0].append(net.start(row_ref.at[core * 16 + there], x_in.at[0, k], "x_" + n))
        along_x[0].append(net.start(row_ref.at[(1 - core) * 16 + there], cross_in.at[k], "c_" + n))
    along_x[0].append(net.start(row_ref.at[(1 - core) * 16 + far + x], from_twin.at[far + x], "twin"))
    twins = []
    for d in offsets[1:]:
        rows = ring(zh, d) * 4
        twins.append(net.start(row_ref.at[pl.ds((1 - core) * 16 + rows, 4)], from_twin.at[pl.ds(rows, 4)], "twin"))
    along_y = [net.start(col_ref.at[pl.ds(ring(y, STEPS[n]) * 2, 2)], y_in.at[k], "y_" + n) for k, n in enumerate(order)]

    for i, d in enumerate(offsets[1:]):
        rows = ring(zh, d) * 4
        twins[i].wait_recv()
        row_sum[pl.ds(rows, 4)] = row_ref[pl.ds(core * 16 + rows, 4)] + from_twin[pl.ds(rows, 4)]
        along_x.append(
            [net.start(row_sum.at[rows + ring(x, STEPS[n])], x_in.at[i + 1, k], "x_" + n) for k, n in enumerate(order)]
        )

    for copy in along_y:
        copy.wait_recv()
    here = y * 2
    col_sum[0] = col_ref[here + 1 - zl] + y_in[0, 1 - zl] + y_in[1, 1 - zl] + y_in[2, 1 - zl]
    pal = net.start(col_sum.at[0], pal_in, "pal")
    col_sum[1] = col_ref[here + zl] + y_in[0, zl] + y_in[1, zl] + y_in[2, zl]

    along_z = []
    for i, d in enumerate(offsets):
        for copy in along_x[i]:
            copy.wait_recv()
        if d == 2:
            total = row_ref[core * 16 + far + x] + from_twin[far + x] + cross_in[0] + cross_in[1] + cross_in[2]
        else:
            total = row_sum[ring(zh, d) * 4 + x]
        total = total + x_in[i, 0] + x_in[i, 1] + x_in[i, 2]
        if d:
            z_out[i] = total
            along_z.append(net.start(z_out.at[i], z_in.at[i], "z_" + order[i]))
        else:
            col_sum[1] = col_sum[1] + total
    pal.wait_recv()
    col_sum[1] = col_sum[1] + pal_in[...]
    for copy in along_z:
        copy.wait_recv()
    col_sum[1] = col_sum[1] + (z_in[0] + z_in[1] + z_in[2])
    for c in range(3):
        for k in range(16):
            out_ref[c : c + 1, k * TILE : (k + 1) * TILE] = col_sum[1, c * 16 + k : c * 16 + k + 1, :]
    net.finish()


def scatter(row_part, col_part):
    vmem = pl.BlockSpec(memory_space=pltpu.VMEM)
    block = lambda *n: pltpu.VMEM((*n, 48, TILE), F32)
    return pl.pallas_call(
        scatter_kernel,
        out_shape=jax.ShapeDtypeStruct((3, 2048), F32),
        in_specs=[vmem, vmem],
        out_specs=vmem,
        scratch_shapes=[
            block(16),
            block(16),
            block(4, 3),
            block(3),
            block(3),
            block(3, 2),
            block(2),
            block(),
            block(3),
            pltpu.SemaphoreType.DMA((SCATTER_COPIES,)),
            pltpu.SemaphoreType.DMA((SCATTER_COPIES,)),
        ],
        compiler_params=pltpu.CompilerParams(
            collective_id=1, has_side_effects=True, vmem_limit_bytes=10 * 1024 * 1024
        ),
        name="scatter_forces",
    )(row_part, col_part)


def shards(positions, type_ids, type_params, pair_tiles, pair_counts):
    tiles, row_data, columns = gather(positions, type_ids.reshape(16, TILE), type_params, pair_tiles[0, 0].T)
    row_part, col_part = forces_of(pair_counts, tiles, row_data, *columns)
    return scatter(row_part, col_part)


def solution(mesh):
    placed = (
        P(None, ("row", "col")),
        P(("row", "col")),
        P(),
        P("row", "col", None, None),
        P("row", "col"),
    )
    return jax.shard_map(
        shards, mesh=mesh, in_specs=placed, out_specs=P(None, ("row", "col")), check_vma=False
    )
```

```python
import math

import jax
import jax.numpy as jnp
from jax import lax
from jax.experimental import pallas as pl
from jax.experimental.pallas import tpu as pltpu
from jax.sharding import PartitionSpec as P

TILE = 128
NTYPES = 16
CUTOFF_SQ = 6.25
LOG2E = math.log2(math.e)
KAPPA = 2.0 / (CUTOFF_SQ * LOG2E)
WIDTH_SCALE = 0.5 / math.sqrt(CUTOFF_SQ * LOG2E)
GROUP = 8
TURNS = 10
CHUNK = 32
UNROLL = GROUP * TURNS
G2 = 2 * GROUP
U2 = GROUP
FIRST = 128
ROW_TILES = 512
COL_TILES = 128
F32 = jnp.float32
BF16 = jnp.bfloat16
MESH = pl.DeviceIdType.MESH


def pieces(value):
    high = value.astype(BF16).astype(F32)
    rest = value - high
    middle = rest.astype(BF16).astype(F32)
    return high, middle, rest, rest - middle


def distance_stack(value, order):
    high, middle, _, low = pieces(value)
    part = {"h": high, "m": middle, "l": low}
    return [jnp.concatenate([part[order[k]], part[order[k + 1]]], axis=0).astype(BF16) for k in (0, 2, 4)]


def moment_stack(value, upper):
    high = value.astype(BF16).astype(F32)
    return jnp.where(upper, high, value - high)


def look_up(table, kind):
    both = jnp.take_along_axis(table, kind.astype(jnp.int32), axis=1)
    return jnp.broadcast_to(both[0:1], (8, TILE)), jnp.broadcast_to(both[4:5], (8, TILE))


def wide(ref, dev, comp, lane):
    return jnp.broadcast_to(ref[dev, comp : comp + 1, pl.ds(lane, TILE)], (8, TILE))


def spread(quad, x, y, z, last):
    return jnp.where(quad == 0, x, jnp.where(quad == 1, y, jnp.where(quad == 2, z, last)))


def column_preparer(table, col_ref, feat, mom, cen, vel, wid):
    sub = lax.broadcasted_iota(jnp.int32, (8, TILE), 0)
    quad = sub & 3
    zero8 = jnp.zeros((8, TILE), F32)
    types = table[...]
    zeros = jnp.zeros((64, TILE), BF16)
    row = lax.broadcasted_iota(jnp.int32, (TILE, TILE), 0)
    pick = jnp.where((row >= 48) & (row < 51), 1.0, 0.0).astype(BF16)

    def prepare(dev, k):
        b = dev * 16 + k
        x, y, z, kind = (wide(col_ref, dev, c, k * TILE) for c in range(4))
        here = spread(quad, x, y, z, 0.0)
        centre = jnp.sum(here, axis=1, keepdims=True) * (1.0 / TILE)
        cen[b] = jnp.broadcast_to(centre, (8, TILE))
        v = here - centre
        norm = jnp.sum(jnp.where(sub < 3, v * v, 0.0), axis=0, keepdims=True)
        depth, width = look_up(types, kind)
        z8 = jnp.where(sub < 3, v * (2.0 / CUTOFF_SQ), jnp.where(sub == 3, 1.0, jnp.where(sub == 4, norm * (-1.0 / CUTOFF_SQ), 0.0)))
        high, middle, _, low = pieces(width)
        widths = jnp.where(sub == 0, high, jnp.where(sub == 1, middle, jnp.where(sub == 2, low, 0.0)))
        widths = jnp.concatenate([widths, zero8], axis=0).astype(BF16)
        turned = jnp.concatenate(distance_stack(z8, "hmlhmh") + [widths, zeros], axis=0).T
        feat[b] = turned
        wid[b] = jnp.dot(turned, pick, preferred_element_type=F32)
        mom[b] = moment_stack(jnp.where(quad == 3, 1.0, v) * depth, sub < 4)
        vel[b] = jnp.where(sub == 3, depth * KAPPA, v)

    def shard(dev):
        for k in range(16):
            prepare(dev, k)

    return shard


def force_kernel(count_ref, tiles_in, row_ref, feat, mom, cen, vel, wid, table, row_out, col_out, acc_row, acc_col, slope, mine, offset, scale, span, reach, tiles_ref, load_sem):
    load_tiles = pltpu.make_async_copy(tiles_in, tiles_ref.at[:, pl.ds(FIRST, 384)], load_sem)
    load_tiles.start()
    sub = lax.broadcasted_iota(jnp.int32, (8, TILE), 0)
    quad = sub & 3
    upper = sub < 4
    unit = jnp.where(sub == 4, 1.0, 0.0)
    types = table[...]
    zeros80 = jnp.zeros((80, TILE), BF16)
    zeros128 = jnp.zeros((TILE, TILE), BF16)
    acc_row[...] = jnp.zeros_like(acc_row)
    acc_col[...] = jnp.zeros_like(acc_col)
    load_tiles.wait()
    count = count_ref[0, 0]
    for k in range(-2 * GROUP, (TURNS + 1) * GROUP):
        at = FIRST + k + (0 if k < 0 else count)
        tiles_ref[0, at] = ROW_TILES
        tiles_ref[1, at] = COL_TILES

    def fold(out):
        return out + pltpu.roll(out, 4, 0)

    def nearness(slot, k):
        a, b = tiles_ref[0, slot] & (ROW_TILES - 1), tiles_ref[1, slot] & (COL_TILES - 1)
        dev = (a & 16) + (a >> 5)
        lane = pl.multiple_of((a & 15) * TILE, TILE)
        x, y, z = (wide(row_ref, dev, c, lane) - jnp.broadcast_to(cen[b, c : c + 1, :], (8, TILE)) for c in range(3))
        kind = wide(row_ref, dev, 3, lane)
        depth, width = look_up(types, kind)
        q = 1.0 - (x * x + y * y + z * z) * (1.0 / CUTOFF_SQ)
        xz = spread(quad, x, y, z, 1.0)
        z8 = jnp.where(sub < 3, xz, jnp.where(sub == 3, q, unit))
        mine[k][...] = moment_stack(xz * depth, upper)
        offset[k][...] = xz
        scale[k][...] = depth * KAPPA
        span[k][...] = width
        return b, jnp.concatenate(distance_stack(z8, "hhhmml") + [zeros80], axis=0)

    def measure(slot, k):
        sides = [nearness(slot + n, k + n) for n in range(2)]
        feats = jnp.concatenate([feat[b] for b, _ in sides], axis=1)
        first, second = (near for _, near in sides)
        weights = jnp.concatenate(
            [jnp.concatenate([first, zeros128], axis=1), jnp.concatenate([zeros128, second], axis=1)], axis=0
        )
        reach[k // 2 % U2][...] = jnp.dot(feats, weights, preferred_element_type=F32)

    def spread_out(slot, k):
        b = tiles_ref[1, slot] & (COL_TILES - 1)
        half = (k % 2) * TILE
        for low in range(0, TILE, CHUNK):
            c = jnp.maximum(reach[k // 2 % U2][low : low + CHUNK, half : half + TILE], 0.0)
            spans = wid[b, low : low + CHUNK, :].reshape(CHUNK // 8, 8, TILE) + span[k][...][None]
            inverse = pl.reciprocal(spans.reshape(CHUNK, TILE), approx=True)
            decay = inverse * inverse
            u = c * decay
            g = (c * (u + 2.0 * LOG2E)) * jnp.exp2(u - decay)
            g_high = g.astype(BF16)
            slope[k % G2][low : low + CHUNK, :] = g_high
            slope[k % G2][TILE + low : TILE + low + CHUNK, :] = (g - g_high.astype(F32)).astype(BF16)

    def gather_in(slot, k):
        a, b = tiles_ref[0, slot], tiles_ref[1, slot]
        a_to, b_to = pl.multiple_of(a * 8, 8), pl.multiple_of(b * 8, 8)
        sides = jnp.concatenate([mom[b & (COL_TILES - 1)], mine[k][...]], axis=0).astype(BF16)
        g = slope[k % G2][...]
        across = jnp.concatenate([g[:TILE].T, g[TILE:].T], axis=0)
        out = jnp.dot(
            jnp.concatenate([sides, sides], axis=1),
            jnp.concatenate([g, across], axis=1),
            preferred_element_type=F32,
        )
        to_i = fold(out[0:8, :TILE])
        to_j = fold(out[8:16, TILE:])
        weight = jnp.broadcast_to(to_i[3:4], (8, TILE))
        on_i = (offset[k][...] * weight - to_i) * scale[k][...]
        return a_to, b_to, on_i, to_j

    def collect(slot, k):
        a_to, b_to, on_i, to_j = gather_in(slot, k)
        acc_row[pl.ds(a_to, 8), :] += on_i
        acc_col[pl.ds(b_to, 8), :] += to_j

    @pl.loop(0, pl.cdiv(pl.cdiv(count, GROUP) + 2, TURNS))
    def _(turn):
        base = FIRST + turn * (TURNS * GROUP)
        for h in range(TURNS):
            for n in range(GROUP):
                collect(base + (h - 2) * GROUP + n, (h - 2) % TURNS * GROUP + n)
                spread_out(base + (h - 1) * GROUP + n, (h - 1) % TURNS * GROUP + n)
                if n % 2:
                    measure(base + h * GROUP + n - 1, h * GROUP + n - 1)

    @pl.loop(0, COL_TILES, step=16)
    def _(b0):
        for k in range(16):
            b = b0 + k
            at = pl.multiple_of(b * 8, 8)
            got = acc_col[pl.ds(at, 8), :]
            v = vel[b]
            weight = jnp.broadcast_to(got[3:4], (8, TILE))
            depth = jnp.broadcast_to(v[3:4], (8, TILE))
            acc_col[pl.ds(at, 8), :] = (v * weight - got) * depth

    for q in range(32):
        slot = (q & 1) * 16 + (q >> 1)
        for c in range(3):
            row_out[slot, c * 16 : c * 16 + 16, :] = acc_row[pl.ds(q * 128 + c, 16, stride=8), :]
    for p in range(8):
        for c in range(3):
            col_out[p, c * 16 : c * 16 + 16, :] = acc_col[pl.ds(p * 128 + c, 16, stride=8), :]


def forces_of(count, tiles, row_data, *columns):
    vmem = pl.BlockSpec(memory_space=pltpu.VMEM)
    return pl.pallas_call(
        force_kernel,
        out_shape=(jax.ShapeDtypeStruct((32, 48, TILE), F32), jax.ShapeDtypeStruct((8, 48, TILE), F32)),
        in_specs=[pl.BlockSpec(memory_space=pltpu.SMEM)] + [vmem] * 8,
        out_specs=(vmem, vmem),
        scratch_shapes=[
            pltpu.VMEM(((ROW_TILES + 1) * 8, TILE), F32),
            pltpu.VMEM(((COL_TILES + 1) * 8, TILE), F32),
            [pltpu.VMEM((2 * TILE, TILE), BF16)] * G2,
            [pltpu.VMEM((8, TILE), F32)] * UNROLL,
            [pltpu.VMEM((8, TILE), F32)] * UNROLL,
            [pltpu.VMEM((8, TILE), F32)] * UNROLL,
            [pltpu.VMEM((8, TILE), F32)] * UNROLL,
            [pltpu.VMEM((TILE, 2 * TILE), F32)] * U2,
            pltpu.SMEM((2, FIRST + 384 + 128), jnp.int32),
            pltpu.SemaphoreType.DMA,
        ],
        compiler_params=pltpu.CompilerParams(vmem_limit_bytes=26 * 1024 * 1024),
        name="pair_forces",
    )(count, tiles, row_data, *columns)


def ring(v, d):
    return (v + d + 4) % 4


def place():
    p, q = lax.axis_index("row"), lax.axis_index("col")
    return p // 2, p % 2, q // 8, (q // 2) % 4, q % 2


def device(y, zl, zh, x, core):
    return (y * 2 + zl, zh * 8 + x * 2 + core)


STEPS = {"far": 2, "up": 1, "down": -1}


def neighbours(y, zl, zh, x, core, cross=False):
    near = {"twin": device(y, zl, zh, x, 1 - core), "pal": device(y, 1 - zl, zh, x, core)}
    for name, d in STEPS.items():
        near["z_" + name] = device(y, zl, ring(zh, d), x, core)
        near["x_" + name] = device(y, zl, zh, ring(x, d), core)
        near["y_" + name] = device(ring(y, d), zl, zh, x, core)
        if cross:
            near["c_" + name] = device(y, zl, zh, ring(x, d), 1 - core)
    return near


def greet(near):
    for target in near.values():
        pl.semaphore_signal(pltpu.get_barrier_semaphore(), inc=1, device_id=target, device_id_type=MESH)


def await_greetings(near):
    pl.semaphore_wait(pltpu.get_barrier_semaphore(), len(near))


class Copies:
    def __init__(self, near, send_sem, recv_sem):
        self.near, self.send_sem, self.recv_sem = near, send_sem, recv_sem
        self.started = []

    def start(self, source, target, to):
        k = len(self.started)
        copy = pltpu.make_async_remote_copy(
            src_ref=source,
            dst_ref=target,
            send_sem=self.send_sem.at[k],
            recv_sem=self.recv_sem.at[k],
            device_id=self.near[to],
            device_id_type=MESH,
        )
        copy.start()
        self.started.append(copy)
        return copy

    def finish(self):
        for copy in self.started:
            copy.wait_send()


GATHER_COPIES = 38
SCATTER_COPIES = 26


def gather_kernel(pos_hbm, type_hbm, params_hbm, tiles_hbm, tiles_ref, row_ref, feat, mom, cen, vel, wid, table, col_ref, params_ref, pos_in, type_in, load_sem, send_sem, recv_sem):
    load_pos = pltpu.make_async_copy(pos_hbm, pos_in, load_sem.at[0])
    load_type = pltpu.make_async_copy(type_hbm, type_in, load_sem.at[1])
    load_params = pltpu.make_async_copy(params_hbm, params_ref, load_sem.at[2])
    load_pos.start()
    load_type.start()
    load_params.start()
    load_tiles = pltpu.make_async_copy(tiles_hbm, tiles_ref, load_sem.at[3])
    load_tiles.start()
    y, zl, zh, x, core = place()
    near = neighbours(y, zl, zh, x, core)
    greet(near)
    at = lambda xx, zz: core * 16 + zz * 4 + xx
    col_at = lambda yy, ll: yy * 2 + ll
    mine, col_mine, col_pal = at(x, zh), col_at(y, zl), col_at(y, 1 - zl)
    load_pos.wait()
    load_type.wait()
    for ref, slot in ((row_ref, mine), (col_ref, col_mine)):
        ref[slot, 0:3, :] = pos_in[...]
        for k in range(16):
            ref[slot, 3:4, k * TILE : (k + 1) * TILE] = type_in[k : k + 1, :].astype(F32)
    await_greetings(near)
    net = Copies(near, send_sem, recv_sem)

    def send(ref, slot, to):
        return net.start(ref.at[slot], ref.at[slot], to)

    along_z = {name: send(row_ref, mine, "z_" + name) for name in STEPS}
    along_x, along_y, twins = {}, {}, []
    pal = send(col_ref, col_mine, "pal")

    def pass_on(zz, key):
        names = ("up", "down") if key in ("up", "down") else STEPS
        along_x[key] = {name: send(row_ref, at(x, zz), "x_" + name) for name in names}
        twins.append(send(row_ref, at(x, zz), "twin"))

    def pass_col(slot, key):
        along_y[key] = {name: send(col_ref, slot, "y_" + name) for name in STEPS}

    def hand_over(zz, key, names):
        for name in names:
            along_x[key][name].wait_recv()
            twins.append(send(row_ref, at(ring(x, -STEPS[name]), zz), "twin"))

    pass_on(zh, "own")
    pass_col(col_mine, 0)
    load_params.wait()
    table[...] = jnp.zeros_like(table)
    for k in range(4):
        table[k : k + 1, 0:NTYPES] = jnp.sqrt(params_ref[0:1, :])
        table[k + 4 : k + 5, 0:NTYPES] = params_ref[1:2, :] * WIDTH_SCALE
    prepare = column_preparer(table, col_ref, feat, mom, cen, vel, wid)
    prepare(col_mine)
    pal.wait_recv()
    pass_col(col_pal, 1)
    along_x["own"]["far"].wait_recv()
    across = {name: send(row_ref, at(ring(x, 2), zh), "z_" + name) for name in ("up", "down")}
    twins.append(send(row_ref, at(ring(x, 2), zh), "twin"))
    for name in ("up", "down"):
        along_z[name].wait_recv()
        pass_on(ring(zh, -STEPS[name]), name)
    hand_over(zh, "own", ("up", "down"))
    prepare(col_pal)
    along_y[0]["up"].wait_recv()
    prepare(col_at(ring(y, -1), zl))
    along_z["far"].wait_recv()
    pass_on(ring(zh, 2), "far")
    along_y[0]["down"].wait_recv()
    prepare(col_at(ring(y, 1), zl))
    along_y[1]["up"].wait_recv()
    prepare(col_at(ring(y, -1), 1 - zl))
    for name in ("up", "down"):
        zz = ring(zh, -STEPS[name])
        hand_over(zz, name, ("up", "down"))
        across[name].wait_recv()
        twins.append(send(row_ref, at(ring(x, 2), zz), "twin"))
    along_y[1]["down"].wait_recv()
    prepare(col_at(ring(y, 1), 1 - zl))
    hand_over(ring(zh, 2), "far", ("up", "down", "far"))
    for key, ll in ((0, zl), (1, 1 - zl)):
        along_y[key]["far"].wait_recv()
        prepare(col_at(ring(y, 2), ll))
    load_tiles.wait()
    for copy in twins:
        copy.wait_recv()
    net.finish()


def in_hbm(array):
    return pltpu.with_memory_space_constraint(array, pltpu.HBM)


def gather(positions, kinds, params, tiles):
    hbm = pl.BlockSpec(memory_space=pltpu.HBM)
    vmem = pl.BlockSpec(memory_space=pltpu.VMEM)
    out = lambda *shape: jax.ShapeDtypeStruct(shape, F32)
    tiles, row_data, *columns = pl.pallas_call(
        gather_kernel,
        out_shape=(
            jax.ShapeDtypeStruct((2, 384), jnp.int32),
            out(32, 4, 2048),
            jax.ShapeDtypeStruct((COL_TILES, TILE, TILE), BF16),
            out(COL_TILES, 8, TILE),
            out(COL_TILES, 8, TILE),
            out(COL_TILES, 8, TILE),
            out(COL_TILES, TILE, TILE),
            out(8, TILE),
        ),
        in_specs=[hbm] * 4,
        out_specs=(vmem,) * 8,
        scratch_shapes=[
            pltpu.VMEM((8, 4, 2048), F32),
            pltpu.VMEM((2, NTYPES), F32),
            pltpu.VMEM((3, 2048), F32),
            pltpu.VMEM((16, TILE), jnp.int32),
            pltpu.SemaphoreType.DMA((4,)),
            pltpu.SemaphoreType.DMA((GATHER_COPIES,)),
            pltpu.SemaphoreType.DMA((GATHER_COPIES,)),
        ],
        compiler_params=pltpu.CompilerParams(
            collective_id=0, has_side_effects=True, vmem_limit_bytes=22 * 1024 * 1024
        ),
        name="gather_atoms",
    )(*map(in_hbm, (positions, kinds, params, tiles)))
    return tiles, row_data, columns


def scatter_kernel(row_ref, col_ref, out_ref, from_twin, row_sum, x_in, z_out, z_in, y_in, col_sum, pal_in, cross_in, send_sem, recv_sem):
    y, zl, zh, x, core = place()
    near = neighbours(y, zl, zh, x, core, cross=True)
    greet(near)
    await_greetings(near)
    net = Copies(near, send_sem, recv_sem)
    offsets = (2, 1, -1, 0)
    order = ("far", "up", "down")

    far = ring(zh, 2) * 4
    along_x = [[]]
    for k, n in enumerate(order):
        there = far + ring(x, STEPS[n])
        along_x[0].append(net.start(row_ref.at[core * 16 + there], x_in.at[0, k], "x_" + n))
        along_x[0].append(net.start(row_ref.at[(1 - core) * 16 + there], cross_in.at[k], "c_" + n))
    along_x[0].append(net.start(row_ref.at[(1 - core) * 16 + far + x], from_twin.at[far + x], "twin"))
    twins = []
    for d in offsets[1:]:
        rows = ring(zh, d) * 4
        twins.append(net.start(row_ref.at[pl.ds((1 - core) * 16 + rows, 4)], from_twin.at[pl.ds(rows, 4)], "twin"))
    along_y = [net.start(col_ref.at[pl.ds(ring(y, STEPS[n]) * 2, 2)], y_in.at[k], "y_" + n) for k, n in enumerate(order)]

    for i, d in enumerate(offsets[1:]):
        rows = ring(zh, d) * 4
        twins[i].wait_recv()
        row_sum[pl.ds(rows, 4)] = row_ref[pl.ds(core * 16 + rows, 4)] + from_twin[pl.ds(rows, 4)]
        along_x.append(
            [net.start(row_sum.at[rows + ring(x, STEPS[n])], x_in.at[i + 1, k], "x_" + n) for k, n in enumerate(order)]
        )

    for copy in along_y:
        copy.wait_recv()
    here = y * 2
    col_sum[0] = col_ref[here + 1 - zl] + y_in[0, 1 - zl] + y_in[1, 1 - zl] + y_in[2, 1 - zl]
    pal = net.start(col_sum.at[0], pal_in, "pal")
    col_sum[1] = col_ref[here + zl] + y_in[0, zl] + y_in[1, zl] + y_in[2, zl]

    along_z = []
    for i, d in enumerate(offsets):
        for copy in along_x[i]:
            copy.wait_recv()
        if d == 2:
            total = row_ref[core * 16 + far + x] + from_twin[far + x] + cross_in[0] + cross_in[1] + cross_in[2]
        else:
            total = row_sum[ring(zh, d) * 4 + x]
        total = total + x_in[i, 0] + x_in[i, 1] + x_in[i, 2]
        if d:
            z_out[i] = total
            along_z.append(net.start(z_out.at[i], z_in.at[i], "z_" + order[i]))
        else:
            col_sum[1] = col_sum[1] + total
    pal.wait_recv()
    col_sum[1] = col_sum[1] + pal_in[...]
    for copy in along_z:
        copy.wait_recv()
    col_sum[1] = col_sum[1] + (z_in[0] + z_in[1] + z_in[2])
    for c in range(3):
        for k in range(16):
            out_ref[c : c + 1, k * TILE : (k + 1) * TILE] = col_sum[1, c * 16 + k : c * 16 + k + 1, :]
    net.finish()


def scatter(row_part, col_part):
    vmem = pl.BlockSpec(memory_space=pltpu.VMEM)
    block = lambda *n: pltpu.VMEM((*n, 48, TILE), F32)
    return pl.pallas_call(
        scatter_kernel,
        out_shape=jax.ShapeDtypeStruct((3, 2048), F32),
        in_specs=[vmem, vmem],
        out_specs=vmem,
        scratch_shapes=[
            block(16),
            block(16),
            block(4, 3),
            block(3),
            block(3),
            block(3, 2),
            block(2),
            block(),
            block(3),
            pltpu.SemaphoreType.DMA((SCATTER_COPIES,)),
            pltpu.SemaphoreType.DMA((SCATTER_COPIES,)),
        ],
        compiler_params=pltpu.CompilerParams(
            collective_id=1, has_side_effects=True, vmem_limit_bytes=10 * 1024 * 1024
        ),
        name="scatter_forces",
    )(row_part, col_part)


def shards(positions, type_ids, type_params, pair_tiles, pair_counts):
    tiles, row_data, columns = gather(positions, type_ids.reshape(16, TILE), type_params, pair_tiles[0, 0].T)
    row_part, col_part = forces_of(pair_counts, tiles, row_data, *columns)
    return scatter(row_part, col_part)


def solution(mesh):
    placed = (
        P(None, ("row", "col")),
        P(("row", "col")),
        P(),
        P("row", "col", None, None),
        P("row", "col"),
    )
    return jax.shard_map(
        shards, mesh=mesh, in_specs=placed, out_specs=P(None, ("row", "col")), check_vma=False
    )
```
